128 devices in a mesh: section: 2 (over core), region: 64 (over x, z, y).
Axes of the slice: x: 4, y: 4, z: 4, core: 2. Of those that a mesh axis runs over, the one named last changes fastest.
Arguments:
- pyramid: bfloat16 [64, 2040, 256], P('region'), may hold values from -6 to 6
- boxes: float32 [4, 8192], P(None, 'region'), may hold values from 0 to 192, as said below
- image_ids: int32 [8192, 1], P('region'), may hold values from 0 to 63; in each aligned block of 64 rows (0 to 63, 64 to 127, ...) at most 2 rows name the same one
- levels: int32 [8192], P('region'), may hold values from 0 to 3, as said below
- labels: int32 [2, 8192], P('section', 'region'), may hold values from 0 to 80
- targets: float32 [2, 4, 8192], P('section', None, 'region'), may hold values from -5 to 5
- w_first: bfloat16 [2, 12544, 1024], P('section'), may hold values from -0.0546875 to 0.0546875
- b_first: float32 [2, 1024], P('section'), may hold values from -3 to 3
- w_second: bfloat16 [2, 1024, 1024], P('section'), may hold values from -0.1875 to 0.1875
- b_second: float32 [2, 1024], P('section'), may hold values from -3 to 3
- w_pred: bfloat16 [2, 85, 1024], P('section'), may hold values from -0.375 to 0.375
- b_pred: float32 [2, 85], P('section'), may hold values from -3 to 3
Outputs:
- grad_first: float32 [2, 12544, 1024], P('section', None, 'region')
- grad_first_bias: float32 [2, 1024], P('section')
- grad_second: float32 [2, 1024, 1024], P('section', None, 'region')
- grad_second_bias: float32 [2, 1024], P('section')
- grad_pred: float32 [2, 85, 1024], P('section', None, 'region')
- grad_pred_bias: float32 [2, 85], P('section')
- grad_pyramid: float32 [2, 64, 2040, 256], P('section', 'region')
- refined_boxes: float32 [2, 4, 8192], P('section', None, 'region')
The draws below stay inside these ranges and needn't reach their ends.
Inputs may be any that keep to these rules, and one draw needn't show every extreme that they name: `image_ids`: image of each region; in each aligned block of 64 regions (the rows of one device's micro-batch) no image is named by more than 2 regions, a bound that some block reaches. `levels`: FPN level of each given box by the usual FPN assignment floor(4 + log2(sqrt(w h) / s0)) - 2, clamped to 0..3, with canonical size s0 = 224 * 32 / 200 pixels; P2 holds most regions. `boxes`: boxes (x1, y1, x2, y2) inside an image of 192 by 128 pixels, with x2 > x1 and y2 > y1.
All inputs are finite; a program needn't handle non-finite values.
Results may differ from the reference program's by a relative error of at most 0.015.
Values may be sent and summed in bfloat16 or wider, within the bound.
No kernel may reach another device: no remote copies, remote signals or barrier semaphores. Data moves between devices by JAX's collectives and lax.ppermute only.
A program may use at most 320 MiB of HBM per device.

```python
import math
import jax
import jax.numpy as jnp
import numpy as np
from jax import lax

C = 256
REP = 1024
CLASSES = 81
R_DEV = 128
MB = 2
H2 = 32
W2 = 48
CELLS = 2040
F = 12544
PRED = 85
CAP = 2
IMAGES = 64
REGIONS = 8192


def region_octaves(key):
    uniform_ints = jax.random.randint(key, (REGIONS,), 0, 10)
    return (uniform_ints >= 6).astype(jnp.int32) + (uniform_ints >= 8).astype(jnp.int32) + (uniform_ints >= 9).astype(jnp.int32)


def draw_levels(key, part):
    octaves = region_octaves(key)
    return octaves


def draw_boxes(key, part):
    octaves = region_octaves(key)
    key = jax.random.fold_in(key, 11)
    subkeys = jax.random.split(key, 4)
    octave_float = octaves.astype(jnp.float32)
    lowest_side = 0.28 * H2 * jnp.exp2(octave_float)
    band_ratio = jnp.where(octaves >= 3, 3.2 / 2.24, 2.0)
    spread = jax.random.uniform(subkeys[0], (REGIONS,), jnp.float32, 0.0, 0.999)
    box_side = lowest_side * jnp.exp(spread * jnp.log(band_ratio))
    aspect = jnp.exp(jax.random.uniform(subkeys[1], (REGIONS,), jnp.float32, -0.18, 0.18))
    box_width = box_side * aspect
    box_height = box_side / aspect
    left_edge = jax.random.uniform(subkeys[2], (REGIONS,), jnp.float32, 0.0, 1.0) * (4.0 * W2 - box_width)
    top_edge = jax.random.uniform(subkeys[3], (REGIONS,), jnp.float32, 0.0, 1.0) * (4.0 * H2 - box_height)
    return jnp.stack([left_edge, top_edge, left_edge + box_width, top_edge + box_height]).astype(jnp.float32)


def set_ends(values, own_key, smallest, largest):
    shape = values.shape
    spot = [jax.random.randint(jax.random.fold_in(own_key, axis), (), 0, shape[axis]) for axis in range(len(shape))]
    values = values.at[tuple(spot)].set(smallest)
    longest = shape.index(max(shape))
    spot[longest] = (spot[longest] + 1) % shape[longest]
    return values.at[tuple(spot)].set(largest)


def level_of(key, shape, cuts, low, largest):
    gain = 1.0
    for position, parts in cuts:
        steps = jax.random.uniform(jax.random.fold_in(jax.random.fold_in(key, 6), position), (parts,), jnp.float32, low / len(cuts), largest / len(cuts))
        gain = gain * jnp.repeat(jnp.exp(steps), shape[position] // parts).reshape((-1,) + (1,) * (len(shape) - 1 - position))
    return gain


def assign_block(rng, own, number, rows, amount, top, most, skew):
    order = jax.random.permutation(rng, amount)
    heavy_load, common = portions_of(amount, rows * top, most, skew, True), portions_of(amount, rows * top, most, skew, False)
    places = jnp.arange(amount)

    def named(lengths, rotation):
        used = int((lengths > 0).sum())
        fixed = max(1, used // 4)
        shifted = fixed + (places - fixed + rotation * (used - fixed)) % max(1, amount - fixed)
        return jnp.zeros((amount,), jnp.int32).at[order[jnp.where(places < fixed, places, shifted)]].set(jnp.asarray(lengths, jnp.int32))

    lengths = jnp.where(number % 4 == 0, named(heavy_load, number // 4), named(common, number - number // 4 - 1))
    mixed = jax.random.permutation(jax.random.fold_in(own, 3), amount)
    donor, sink = mixed[0:amount // 2 * 2:2], mixed[1:amount // 2 * 2:2]
    margin = jnp.minimum(lengths[donor] - 1, most - lengths[sink]) // 2
    margin = jnp.where((donor == order[0]) | (sink == order[0]) | (lengths[sink] == 0), 0, jnp.maximum(margin, 0))
    shifted = jax.random.randint(jax.random.fold_in(own, 4), (amount // 2,), 0, 1 << 20) % (margin + 1)
    lengths = lengths.at[donor].add(-shifted).at[sink].add(shifted)
    items = jnp.searchsorted(jnp.cumsum(lengths), jnp.arange(rows * top), side="right").astype(jnp.int32)
    grid = items.reshape(top, rows).T
    grid = grid[jax.random.permutation(jax.random.fold_in(own, 1), rows)]
    rotation = jax.random.randint(jax.random.fold_in(own, 2), (rows, 1), 0, top)
    return jnp.take_along_axis(grid, (jnp.arange(top)[None, :] + rotation) % top, axis=1)


def portions_of(count, total, bound, lean, full):
    portions = [(1 << 20) // math.isqrt(rank ** lean) + 1 for rank in range(1, count + 1)]
    largest = bound if full else min(bound, max(-(-total // count), total * portions[0] // sum(portions)))
    least = 1 if total - largest >= count - 1 else 0
    given, surplus = [largest] + [least] * (count - 1), total - largest - least * (count - 1)
    while surplus > 0:
        movable = [i for i in range(1, count) if given[i] < largest] or [i for i in range(1, count) if given[i] < bound]
        pool, left = sum([portions[i] for i in movable]), surplus
        for i in movable:
            extra = min(bound - given[i], max(1, left * portions[i] // pool), surplus)
            given[i] = given[i] + extra
            surplus = surplus - extra
    return np.array(given)


def normal_values(stream_key, shape, scale, reach, cuts=(), kind=jnp.bfloat16):
    drawn = scale * jax.random.normal(stream_key, shape, jnp.float32)
    if cuts:
        drawn = drawn * level_of(stream_key, shape, cuts, -0.22, 0.18)
    return jnp.clip(drawn, -reach, reach).astype(kind)


def setup_inputs(seed: int = 0) -> dict:
    seeds = jax.random.split(jax.random.key(seed), 13)
    pyramid = normal_values(seeds[0], (IMAGES, CELLS, C), 1.0, 6.0, ((0, 64),))
    boxes = draw_boxes(jax.random.fold_in(seeds[12], 71), 0)
    image_ids_keys = jax.random.split(jax.random.fold_in(seeds[2], 1), REGIONS // (R_DEV // MB))
    image_ids_turns = jax.random.permutation(jax.random.fold_in(seeds[2], 3), REGIONS // (R_DEV // MB))
    image_ids = jax.vmap(lambda own, number: assign_block(jax.random.fold_in(seeds[2], 2), own, number, R_DEV // MB, IMAGES, 1, CAP, 2))(image_ids_keys, image_ids_turns).reshape((REGIONS, 1))
    levels = draw_levels(jax.random.fold_in(seeds[12], 71), 0)
    labels = set_ends(jax.random.randint(seeds[4], (2, REGIONS), 0, CLASSES), jax.random.fold_in(seeds[4], 1), 0, CLASSES - 1).astype(jnp.int32)
    targets = normal_values(seeds[5], (2, 4, REGIONS), 1.0, 5.0, ((0, 2), (2, 64)), jnp.float32)
    w_first = normal_values(seeds[6], (2, F, REP), F ** -0.5, 0.0546875, ((0, 2),))
    b_first = normal_values(seeds[7], (2, REP), 0.5, 3.0, ((0, 2),), jnp.float32)
    w_second = normal_values(seeds[8], (2, REP, REP), REP ** -0.5, 0.1875, ((0, 2),))
    b_second = normal_values(seeds[9], (2, REP), 0.5, 3.0, ((0, 2),), jnp.float32)
    w_pred = normal_values(seeds[10], (2, PRED, REP), (REP // 4) ** -0.5, 0.375, ((0, 2),))
    b_pred = normal_values(seeds[11], (2, PRED), 0.5, 3.0, ((0, 2),), jnp.float32)
    return {"pyramid": pyramid, "boxes": boxes, "image_ids": image_ids, "levels": levels, "labels": labels, "targets": targets, "w_first": w_first, "b_first": b_first, "w_second": w_second, "b_second": b_second, "w_pred": w_pred, "b_pred": b_pred}


@jax.custom_vjp
def low(v):
    return lax.optimization_barrier(v.astype(jnp.bfloat16)).astype(jnp.float32)

@jax.custom_vjp
def low_back(v):
    return v

def low_keep(v):
    return (low(v), None)

def low_pass(kept, grad):
    return (grad,)

def back_keep(v):
    return (v, None)

def back_low(kept, grad):
    return (low(grad),)
low.defvjp(low_keep, low_pass)
low_back.defvjp(back_keep, back_low)
exact_precision = lax.Precision.HIGHEST

def gelu_curve(values):
    return jax.nn.gelu(values, approximate=True)

def level_tables():
    heights = [H2 // 2 ** octave for octave in range(4)]
    widths = [W2 // 2 ** octave for octave in range(4)]
    offsets = [sum((heights[before] * widths[before] for before in range(octave))) for octave in range(4)]
    strides = [4.0 * 2 ** octave for octave in range(4)]
    return (jnp.array(heights, dtype=jnp.int32), jnp.array(widths, dtype=jnp.int32), jnp.array(offsets, dtype=jnp.int32), jnp.array(strides, dtype=jnp.float32))

def level_pick(levels, values):
    chosen = levels[:, None] == jnp.arange(4, dtype=jnp.int32)[None, :]
    return lax.optimization_barrier(jnp.sum(jnp.where(chosen, values[None, :], jnp.zeros_like(values)[None, :]), axis=1, dtype=values.dtype))

def sample_axis(lower_edge, upper_edge, stride, extent):
    offsets_in_bin = (jnp.arange(14, dtype=jnp.float32) + 0.5) / 2.0
    anchor = lower_edge / stride - 0.5
    bin_size = (upper_edge - lower_edge) / stride / 7.0
    coords = anchor[:, None] + bin_size[:, None] * offsets_in_bin[None, :]
    coords = jnp.clip(coords, 0.0, (extent - 1).astype(jnp.float32)[:, None])
    floors = jnp.floor(coords)
    lower_cell = floors.astype(jnp.int32)
    upper_cell = jnp.minimum(lower_cell + 1, extent[:, None] - 1)
    upper_share = coords - floors
    return (jnp.stack([lower_cell, upper_cell], axis=-1), jnp.stack([1.0 - upper_share, upper_share], axis=-1))

def sample_taps(corners, levels, live, first_cell):
    heights, widths, offsets, strides = level_tables()
    stride = level_pick(levels, strides)
    height = level_pick(levels, heights)
    width = level_pick(levels, widths)
    offset = level_pick(levels, offsets)
    row_cells, row_shares = sample_axis(corners[1], corners[3], stride, height)
    col_cells, col_shares = sample_axis(corners[0], corners[2], stride, width)
    slot_total = corners.shape[1]
    base_cell = (first_cell + offset)[:, None, None, None, None]
    tap_cells = base_cell + row_cells[:, :, None, :, None] * width[:, None, None, None, None] + col_cells[:, None, :, None, :]
    tap_shares = row_shares[:, :, None, :, None] * col_shares[:, None, :, None, :] * (0.25 * live)[:, None, None, None, None]
    return (tap_cells.reshape(slot_total, 7, 2, 7, 2, 4), tap_shares.reshape(slot_total, 7, 2, 7, 2, 4))

def roi_pool(feature_table, tap_cells, tap_shares):
    picked = feature_table[tap_cells].astype(jnp.float32)
    pooled = jnp.einsum('spiqjkc,spiqjk->spqc', picked, tap_shares, precision=exact_precision)
    return pooled.reshape(pooled.shape[0], -1)

def decode_boxes(corners, deltas, scales):
    widths = corners[2] - corners[0]
    heights = corners[3] - corners[1]
    center_x = corners[0] + 0.5 * widths
    center_y = corners[1] + 0.5 * heights
    new_x = center_x + deltas[:, 0] / scales[0] * widths
    new_y = center_y + deltas[:, 1] / scales[1] * heights
    new_width = widths * jnp.exp(deltas[:, 2] / scales[2])
    new_height = heights * jnp.exp(deltas[:, 3] / scales[3])
    return jnp.stack([new_x - 0.5 * new_width, new_y - 0.5 * new_height, new_x + 0.5 * new_width, new_y + 0.5 * new_height])

def head_loss(weights, pooled, labels, targets, factor):
    first_weight, first_bias, second_weight, second_bias, pred_weight, pred_bias = weights
    pooled = low_back(low(pooled))
    pre_first = low_back(jnp.dot(pooled, first_weight, precision=exact_precision, preferred_element_type=jnp.float32) + first_bias)
    act_first = low(gelu_curve(pre_first))
    pre_second = low_back(jnp.dot(act_first, second_weight, precision=exact_precision, preferred_element_type=jnp.float32) + second_bias)
    act_second = low(gelu_curve(pre_second))
    outputs = low_back(jnp.dot(act_second, pred_weight.T, precision=exact_precision, preferred_element_type=jnp.float32) + pred_bias)
    logits = outputs[:, :CLASSES]
    deltas = outputs[:, CLASSES:]
    truth = labels[:, None] == jnp.arange(CLASSES, dtype=jnp.int32)[None, :]
    entropy = jax.nn.logsumexp(logits, axis=1) - lax.optimization_barrier(jnp.sum(jnp.where(truth, logits, jnp.zeros_like(logits)), axis=1))
    residue = deltas - targets.T
    huber_terms = jnp.where(jnp.abs(residue) < 1.0, 0.5 * residue * residue, jnp.abs(residue) - 0.5)
    foreground = (labels > 0).astype(jnp.float32)
    return (factor * (jnp.sum(entropy) + jnp.sum(foreground[:, None] * huber_terms)), deltas)

def section_loss(weights, feature_table, corners, images, levels, labels, targets, factor):
    block_rows = R_DEV // MB
    blocks = REGIONS // block_rows

    def one_block(pieces):
        block_corners, block_images, block_levels, block_labels, block_targets = pieces
        live = jnp.ones((block_rows,), jnp.float32)
        tap_cells, tap_shares = sample_taps(block_corners, block_levels, live, block_images * CELLS)
        pooled = roi_pool(feature_table, tap_cells, tap_shares)
        return head_loss(weights, pooled, block_labels, block_targets, factor)
    pieces = (corners.reshape(4, blocks, block_rows).transpose(1, 0, 2), images.reshape(blocks, block_rows), levels.reshape(blocks, block_rows), labels.reshape(blocks, block_rows), targets.reshape(4, blocks, block_rows).transpose(1, 0, 2))
    losses, deltas = lax.map(jax.checkpoint(one_block), pieces)
    return (jnp.sum(losses), deltas.reshape(REGIONS, 4))

def reference(pyramid, boxes, image_ids, levels, labels, targets, w_first, b_first, w_second, b_second, w_pred, b_pred):
    feature_table = pyramid.astype(jnp.float32).reshape(IMAGES * CELLS, C)
    images = image_ids[:, 0]
    params = tuple((array.astype(jnp.float32) for array in (w_first, b_first, w_second, b_second, w_pred, b_pred)))

    def section_weights(weights, section_number):
        return tuple((array[section_number] for array in weights))
    first_scales = (10.0, 10.0, 5.0, 5.0)
    second_scales = (20.0, 20.0, 10.0, 10.0)
    unused_loss, first_deltas = section_loss(section_weights(params, 0), feature_table, boxes, images, levels, labels[0], targets[0], 1.0)
    second_boxes = decode_boxes(boxes, first_deltas, first_scales)

    def total_loss(weights, table_one, table_two):
        loss_one, unused_deltas = section_loss(section_weights(weights, 0), table_one, boxes, images, levels, labels[0], targets[0], 1.0)
        loss_two, deltas_two = section_loss(section_weights(weights, 1), table_two, second_boxes, images, levels, labels[1], targets[1], 0.5)
        return (loss_one + loss_two, deltas_two)
    loss_value, pullback, second_deltas = jax.vjp(total_loss, params, feature_table, feature_table, has_aux=True)
    gradients, grad_one, grad_two = pullback(jnp.ones_like(loss_value))
    final_boxes = decode_boxes(second_boxes, second_deltas, second_scales)
    grad_pyramid = jnp.stack([grad_one, grad_two]).reshape(2, IMAGES, CELLS, C)
    refined_boxes = jnp.stack([second_boxes, final_boxes])
    return (gradients[0], gradients[1], gradients[2], gradients[3], gradients[4], gradients[5], grad_pyramid, refined_boxes)
```

```python
import jax
import jax.numpy as jnp
import numpy as np
from jax import lax
from jax.experimental import pallas as pl
from jax.experimental.pallas import tpu as pltpu
from jax.sharding import PartitionSpec as P

SIDE = 4
GROUPS = 64
SLOTS = 256
GROUP = 16
SLOT_QUARTER = 64
REGIONS = 128
CHANNELS = 256
BINS = 49
FEATURES = 12544
HIDDEN = 1024
CLASSES = 81
PRED = 85
PART_Y = 1280
PART_Z = 1920
SPLIT = SIDE * PART_Y
WIDE = SPLIT + SIDE * PART_Z
EXTRA = HIDDEN + 128
TAIL = 16
WIDE_Y = PART_Y + EXTRA
CELLS = 2040
CELLS_PAD = 2048
EXACT = lax.Precision.HIGHEST
F32 = jnp.float32
BF16 = jnp.bfloat16
HBM = pl.BlockSpec(memory_space=pltpu.HBM)
VMEM = pl.BlockSpec(memory_space=pltpu.VMEM)
SMEM = pl.BlockSpec(memory_space=pltpu.SMEM)
MIB = 1 << 20
PARAMS = pltpu.CompilerParams(vmem_limit_bytes=60 * MIB)
SMALL = pltpu.CompilerParams(vmem_limit_bytes=16 * MIB)

BOX, LEVEL, LABEL, TARGET, LIVE = 0, 4, 5, 6, 10
FIELDS = 16


def ring_pairs(axis, by):
    step = {"x": 16, "z": 4, "y": 1}[axis]
    pairs = []
    for source in range(GROUPS):
        place = source // step % SIDE
        pairs.append((source, source + ((place + by) % SIDE - place) * step))
    return pairs


def shift(array, axis, by):
    return lax.ppermute(array, "region", ring_pairs(axis, by))


def coordinates():
    own = lax.axis_index("region")
    return own // 16, own // 4 % SIDE, own % SIDE


def cell_tables():
    rows = np.full((CELLS_PAD,), -1000.0, np.float32)
    cols = np.full((CELLS_PAD,), -1000.0, np.float32)
    levels = np.full((CELLS_PAD,), -1.0, np.float32)
    start = 0
    for octave in range(4):
        height, width = 32 >> octave, 48 >> octave
        spots = np.arange(height * width)
        rows[start : start + height * width] = 0.5 * (spots // width)
        cols[start : start + height * width] = 0.5 * (spots % width)
        levels[start : start + height * width] = octave
        start += height * width
    return rows, cols, levels


def tent_pair(first, second, cells):
    return jnp.maximum(0.5 - jnp.abs(first - cells), 0.0) + jnp.maximum(
        0.5 - jnp.abs(second - cells), 0.0
    )


def sample_coordinates(records):
    lane = lax.broadcasted_iota(jnp.int32, records.shape, 1)
    level = records[:, LEVEL : LEVEL + 1]

    def of_level(values):
        return jnp.where(
            level == 0.0,
            values[0],
            jnp.where(level == 1.0, values[1], jnp.where(level == 2.0, values[2], values[3])),
        ).astype(F32)

    scale = of_level((0.25, 0.125, 0.0625, 0.03125))
    anchors, bins = [], []
    for low in (1, 0):
        lower, upper = records[:, low : low + 1], records[:, low + 2 : low + 3]
        anchors.append(lower * scale - 0.5)
        bins.append((upper - lower) * scale / 7.0)
    along_y = lane < 16
    offset = (jnp.where(along_y, lane, lane - 16).astype(F32) + 0.5) * 0.5
    coords = jnp.where(along_y, anchors[0], anchors[1]) + jnp.where(along_y, bins[0], bins[1]) * offset
    limit = jnp.where(along_y, of_level((31.0, 15.0, 7.0, 3.0)), of_level((47.0, 23.0, 11.0, 5.0)))
    return 0.5 * jnp.minimum(jnp.maximum(coords, 0.0), limit)


def row_window(coords, wanted):
    lane = lax.broadcasted_iota(jnp.int32, coords.shape, 1)
    mine = wanted & (lane < 14)
    low = jnp.min(jnp.where(mine, coords, 1000.0))
    high = jnp.max(jnp.where(mine, coords, -1000.0))
    first = (2.0 * low).astype(jnp.int32)
    return first, (2.0 * high).astype(jnp.int32) + 2 - first


def slot_of_regions(images):
    lane = lax.broadcasted_iota(jnp.int32, (1, REGIONS), 1)
    wide = jnp.broadcast_to(images, (REGIONS, REGIONS))
    row = lax.broadcasted_iota(jnp.int32, (REGIONS, REGIONS), 0)
    column = lax.broadcasted_iota(jnp.int32, (REGIONS, REGIONS), 1)
    earlier = (wide.T == wide) & (row < column) & ((row >= 64) == (column >= 64))
    second = jnp.max(jnp.where(earlier, 1.0, 0.0), axis=0, keepdims=True)
    return jnp.where(lane >= 64, 2.0, 0.0) + second


def send_kernel(image_ref, box_ref, level_ref, label_ref, target_ref, out_ref):
    images = image_ref[...].astype(F32)
    slots = slot_of_regions(images)
    fields = jnp.concatenate(
        [
            box_ref[...],
            level_ref[...].astype(F32),
            label_ref[...].astype(F32),
            target_ref[...],
            jnp.ones((1, REGIONS), F32),
            jnp.zeros((5, REGIONS), F32),
        ],
        axis=0,
    )
    owner = lax.broadcasted_iota(jnp.int32, (GROUPS, REGIONS), 0).astype(F32) == images
    out_ref[...] = jnp.zeros_like(out_ref)
    for c in range(4):
        chosen = jnp.where(owner & (slots == float(c)), 1.0, 0.0)
        out_ref[:, c * FIELDS : (c + 1) * FIELDS] = lax.dot_general(
            chosen, fields, (((1,), (1,)), ((), ())), precision=EXACT, preferred_element_type=F32
        )


def send_regions(images, boxes, levels, labels, targets):
    return pl.pallas_call(
        send_kernel,
        out_shape=jax.ShapeDtypeStruct((GROUPS, 128), F32),
        in_specs=[VMEM] * 5,
        out_specs=VMEM,
        compiler_params=SMALL,
        cost_estimate=pl.CostEstimate(flops=10**7, bytes_accessed=10**5, transcendentals=0),
        name="send_regions",
    )(images, boxes, levels, labels, targets)


def select_kernel(got_ref, record_ref, place_ref, count_ref, raw_ref):
    raw_ref[...] = jnp.zeros_like(raw_ref)
    for c in range(4):
        raw_ref[c * GROUPS : (c + 1) * GROUPS, :FIELDS] = got_ref[
            :, c * FIELDS : (c + 1) * FIELDS
        ]
    raw = raw_ref[...]
    lane = lax.broadcasted_iota(jnp.int32, (SLOTS, 128), 1)
    raw = jnp.where((lane == LEVEL) & (raw[:, LIVE : LIVE + 1] == 0.0), 4.0, raw)
    turned = raw.T
    spot_col = lax.broadcasted_iota(jnp.int32, (SLOTS, 1), 0).astype(F32)
    spot_row = lax.broadcasted_iota(jnp.int32, (1, SLOTS), 1).astype(F32)
    levels_row = turned[LEVEL : LEVEL + 1, :]
    key_col = raw[:, LEVEL : LEVEL + 1] * 1024.0 + raw[:, 1:2] + raw[:, 3:4]
    key_row = levels_row * 1024.0 + turned[1:2, :] + turned[3:4, :]
    same = key_col == key_row
    col_first = (key_col < key_row) | (same & (spot_col < spot_row))
    row_first = (key_row < key_col) | (same & (spot_row < spot_col))
    place_row = jnp.sum(jnp.where(col_first, 1.0, 0.0), axis=0, keepdims=True)
    place_col = jnp.sum(jnp.where(row_first, 1.0, 0.0), axis=1, keepdims=True)
    order = jnp.where(
        lax.broadcasted_iota(jnp.int32, (SLOTS, SLOTS), 0).astype(F32) == place_row, 1.0, 0.0
    )
    record_ref[...] = jnp.dot(order, raw, precision=EXACT, preferred_element_type=F32)
    place_ref[...] = jnp.broadcast_to(place_col, (SLOTS, 128))
    for octave in range(4):
        count_ref[octave] = jnp.sum(jnp.where(levels_row <= float(octave), 1, 0))


def select_slots(got):
    return pl.pallas_call(
        select_kernel,
        out_shape=(
            jax.ShapeDtypeStruct((SLOTS, 128), F32),
            jax.ShapeDtypeStruct((SLOTS, 128), F32),
            jax.ShapeDtypeStruct((8,), jnp.int32),
        ),
        in_specs=[VMEM],
        out_specs=(VMEM, VMEM, SMEM),
        scratch_shapes=[pltpu.VMEM((SLOTS, 128), F32)],
        compiler_params=SMALL,
        cost_estimate=pl.CostEstimate(flops=10**8, bytes_accessed=10**6, transcendentals=0),
        name="select_slots",
    )(got)


def gelu(values):
    inner = 0.7978845608028654 * (values + 0.044715 * (values * values * values))
    return 0.5 * values * (1.0 + jnp.tanh(inner))


def gelu_slope(values):
    square = values * values
    inner = 0.7978845608028654 * values * (1.0 + 0.044715 * square)
    bend = jnp.tanh(inner)
    slope = 0.7978845608028654 * (1.0 + 3.0 * 0.044715 * square)
    return 0.5 * (1.0 + bend) + 0.5 * values * (1.0 - bend * bend) * slope


PIECE = 1792
PIECES = FEATURES // PIECE


def pool_all(count_ref, records, map_ref, table_ref, coord_ref, level_ref, weight_ref, total_ref, pooled_ref):
    def level_block(first_cell, cells, period, coords, wanted, first_row=None):
        map_rows = slice(first_cell, first_cell + cells)
        if first_row is not None:
            map_rows = pl.ds(pl.multiple_of(first_row * 48, 16), cells)
            lane = lax.broadcasted_iota(jnp.int32, coords.shape, 1)
            coords = jnp.where(lane < 16, coords - 0.5 * first_row.astype(F32), coords)
        row_cells = table_ref[0:1, first_cell : first_cell + cells]
        col_cells = table_ref[1:2, first_cell : first_cell + period]
        columns = []
        for q in range(7):
            share = tent_pair(
                coords[:, 16 + 2 * q : 17 + 2 * q], coords[:, 17 + 2 * q : 18 + 2 * q], col_cells
            )
            columns.append(jnp.where(wanted, share, 0.0).astype(BF16))
        for p in range(7):
            share = tent_pair(
                coords[:, 2 * p : 2 * p + 1], coords[:, 2 * p + 1 : 2 * p + 2], row_cells
            ).astype(BF16)
            for q in range(7):
                for part in range(cells // period):
                    weight_ref[
                        (p * 7 + q) * GROUP : (p * 7 + q + 1) * GROUP,
                        part * period : (part + 1) * period,
                    ] = share[:, part * period : (part + 1) * period] * columns[q]
        total_ref[...] += jnp.dot(
            weight_ref[:, :cells],
            map_ref[map_rows, :],
            preferred_element_type=F32,
        )

    coord_ref[...] = sample_coordinates(records)
    level_ref[...] = jnp.broadcast_to(records[:, LEVEL : LEVEL + 1], level_ref.shape)
    up_to = [count_ref[octave] for octave in range(4)]
    live_groups = (up_to[3] + GROUP - 1) // GROUP
    pooled_ref[:, FEATURES:] = jnp.zeros((SLOTS, WIDE - FEATURES), BF16)

    def dead_group(group, carry):
        pooled_ref[pl.ds(pl.multiple_of(group * GROUP, GROUP), GROUP), :FEATURES] = jnp.zeros(
            (GROUP, FEATURES), BF16
        )
        return carry

    lax.fori_loop(live_groups, SLOTS // GROUP, dead_group, 0)

    def one_group(group, carry):
        start = pl.multiple_of(group * GROUP, GROUP)
        rows = pl.ds(start, GROUP)
        total_ref[...] = jnp.zeros_like(total_ref)

        @pl.when(start < up_to[0])
        def _():
            coords = coord_ref[rows, :]
            wanted = level_ref[rows, 0:1] == 0.0
            first, count = row_window(coords, wanted)

            @pl.when(count <= 10)
            def _():
                level_block(0, 512, 512, coords, wanted, jnp.minimum(first, 22))

            @pl.when((count > 10) & (count <= 16))
            def _():
                level_block(0, 768, 384, coords, wanted, jnp.minimum(first, 16))

            @pl.when(count > 16)
            def _():
                level_block(0, 1536, 384, coords, wanted)

        @pl.when((start + GROUP > up_to[0]) & (start < up_to[1]))
        def _():
            level_block(1536, 384, 384, coord_ref[rows, :], level_ref[rows, 0:1] == 1.0)

        @pl.when((start + GROUP > up_to[1]) & (start < up_to[3]))
        def _():
            level_block(
                1920, 128, 128, coord_ref[rows, :], level_ref[rows, :] == table_ref[2:3, 1920:2048]
            )

        for spot in range(BINS):
            pooled_ref[rows, spot * CHANNELS : (spot + 1) * CHANNELS] = total_ref[
                spot * GROUP : (spot + 1) * GROUP, :
            ].astype(BF16)
        return carry

    lax.fori_loop(0, live_groups, one_group, 0)


def pooled_copies(pooled_ref, others, sems, way, start):
    own_x, own_z, own_y = coordinates()
    for part, (own, width, first) in enumerate(((own_y, PART_Y, 0), (own_z, PART_Z, SPLIT))):
        for chunk in range(SIDE):
            here = pooled_ref.at[:, first + chunk * width : first + (chunk + 1) * width]

            def copy(place):
                there = others[part * SIDE + place]
                ends = (here, there) if way == "out" else (there, here)
                return pltpu.make_async_copy(*ends, sems.at[part, chunk])

            if not start:
                copy(0).wait()
                continue
            for place in range(SIDE):

                @pl.when((own + place) % SIDE == chunk)
                def _():
                    copy(place).start()


def own_records(record_ref, box_ref):
    lane = lax.broadcasted_iota(jnp.int32, record_ref.shape, 1)
    return jnp.where(lane < 4, box_ref[...], record_ref[...])


def weight_copy(w1_ref, w1_buf, sems, piece):
    rows = pl.ds(pl.multiple_of(piece * PIECE, PIECE), PIECE)
    return pltpu.make_async_copy(w1_ref.at[rows, :], w1_buf.at[rows, :], sems.at[piece])


def first_layer(pooled_ref, w1_ref, w1_buf, sems, b1_ref, pre1, ready):
    pre1[...] = jnp.broadcast_to(b1_ref[...], pre1.shape)

    def one_piece(piece, carry):
        ready(piece)
        weight_copy(w1_ref, w1_buf, sems, piece).wait()
        columns = pl.ds(pl.multiple_of(piece * PIECE, PIECE), PIECE)
        pre1[...] += jnp.dot(pooled_ref[:, columns], w1_buf[columns, :], preferred_element_type=F32)
        return carry

    lax.fori_loop(0, PIECES, one_piece, 0)


def later_layers(
    section, records, pre1, pre2, act1, act2, pred, next_ref, w2_ref, b2_ref, wp_ref, bp_ref, done
):
    done(0)
    act1[...] = gelu(pre1[...]).astype(BF16)
    done(2)
    pre2[...] = jnp.dot(act1[...], w2_ref[...], preferred_element_type=F32) + b2_ref[...]
    done(1)
    act2[...] = gelu(pre2[...]).astype(BF16)
    done(3)
    pred[...] = (
        lax.dot_general(act2[...], wp_ref[...], (((1,), (1,)), ((), ())), preferred_element_type=F32)
        + bp_ref[...]
    )
    done(4)
    lane = lax.broadcasted_iota(jnp.int32, records.shape, 1)
    x1, y1, x2, y2 = [records[:, BOX + k : BOX + k + 1] for k in range(4)]
    deltas = [pred[:, CLASSES + k : CLASSES + k + 1] for k in range(4)]
    near, far = (10.0, 5.0) if section == 0 else (20.0, 10.0)
    width, height = x2 - x1, y2 - y1
    center_x, center_y = x1 + 0.5 * width, y1 + 0.5 * height
    new_x = center_x + deltas[0] / near * width
    new_y = center_y + deltas[1] / near * height
    new_width = width * jnp.exp(deltas[2] / far)
    new_height = height * jnp.exp(deltas[3] / far)
    corners = (
        new_x - 0.5 * new_width,
        new_y - 0.5 * new_height,
        new_x + 0.5 * new_width,
        new_y + 0.5 * new_height,
    )
    result = jnp.zeros_like(records)
    for k in range(4):
        result = jnp.where(lane == BOX + k, corners[k], result)
    next_ref[...] = result


KEPT = [((SLOTS, HIDDEN), F32)] * 2 + [((SLOTS, HIDDEN), BF16)] * 2 + [((SLOTS, 128), F32)]
POOL_SCRATCH = [
    pltpu.VMEM((SLOTS, 128), F32),
    pltpu.VMEM((SLOTS, 128), F32),
    pltpu.VMEM((BINS * GROUP, 1536), BF16),
    pltpu.VMEM((BINS * GROUP, CHANNELS), F32),
]
POOLED_SCRATCH = [pltpu.VMEM((SLOTS, WIDE), BF16), pltpu.SemaphoreType.DMA((2, SIDE))]
POOLED = [((SLOTS, PART_Y), BF16)] * SIDE + [((SLOTS, PART_Z), BF16)] * SIDE
HEAD_SCRATCH = [
    pltpu.VMEM((FEATURES, HIDDEN), BF16),
    pltpu.VMEM((SLOTS, HIDDEN), F32),
    pltpu.VMEM((SLOTS, HIDDEN), F32),
    pltpu.VMEM((SLOTS, HIDDEN), BF16),
    pltpu.VMEM((SLOTS, HIDDEN), BF16),
    pltpu.VMEM((SLOTS, 128), F32),
    pltpu.SemaphoreType.DMA((PIECES,)),
    pltpu.SemaphoreType.DMA((5,)),
]


def forward_kernel(
    count_ref,
    record_ref,
    map_ref,
    table_ref,
    b1_ref,
    w2_ref,
    b2_ref,
    wp_ref,
    bp_ref,
    w1_ref,
    *refs,
):
    parts, kept_out, next_ref = refs[: 2 * SIDE], refs[2 * SIDE : 2 * SIDE + 5], refs[2 * SIDE + 5]
    refs = refs[2 * SIDE + 6 :]
    pool_scratch, refs = refs[:4], refs[4:]
    pooled_ref, pooled_sems, w1_buf, pre1, pre2, act1, act2, pred, w_sems, sems = refs

    @pl.when(lax.axis_index("section") == 0)
    def _():
        for piece in range(PIECES):
            weight_copy(w1_ref, w1_buf, w_sems, piece).start()
        records = record_ref[...]
        pool_all(count_ref, records, map_ref, table_ref, *pool_scratch, pooled_ref)
        pooled_copies(pooled_ref, parts, pooled_sems, "out", True)
        first_layer(pooled_ref, w1_ref, w1_buf, w_sems, b1_ref, pre1, lambda piece: None)
        copies = [
            pltpu.make_async_copy(here, there, sems.at[place])
            for place, (here, there) in enumerate(zip((pre1, pre2, act1, act2, pred), kept_out))
        ]
        later_layers(
            0,
            records,
            pre1,
            pre2,
            act1,
            act2,
            pred,
            next_ref,
            w2_ref,
            b2_ref,
            wp_ref,
            bp_ref,
            lambda place: copies[place].start(),
        )
        for copy in copies:
            copy.wait()
        pooled_copies(pooled_ref, parts, pooled_sems, "out", False)


def run_forward(counts, records, feature_map, table, weights):
    kept = POOLED + KEPT
    return pl.pallas_call(
        forward_kernel,
        out_shape=tuple(jax.ShapeDtypeStruct(*entry) for entry in kept)
        + (jax.ShapeDtypeStruct((SLOTS, 128), F32),),
        in_specs=[SMEM] + [VMEM] * 8 + [HBM],
        out_specs=(HBM,) * len(kept) + (VMEM,),
        scratch_shapes=POOL_SCRATCH + POOLED_SCRATCH + HEAD_SCRATCH,
        compiler_params=PARAMS,
        cost_estimate=pl.CostEstimate(
            flops=16 * 10**9, bytes_accessed=36 * 10**6, transcendentals=5 * 10**5
        ),
        name="run_forward",
    )(counts, records, feature_map, table, *weights)


def pool_kernel(count_ref, record_ref, box_ref, map_ref, table_ref, *refs):
    parts = refs[2 * SIDE : 4 * SIDE]
    *pool_scratch, pooled_ref, pooled_sems = refs[4 * SIDE :]

    @pl.when(lax.axis_index("section") == 1)
    def _():
        records = own_records(record_ref, box_ref)
        pool_all(count_ref, records, map_ref, table_ref, *pool_scratch, pooled_ref)
        pooled_copies(pooled_ref, parts, pooled_sems, "out", True)
        pooled_copies(pooled_ref, parts, pooled_sems, "out", False)


def run_pool(counts, records, boxes, feature_map, table, before):
    return pl.pallas_call(
        pool_kernel,
        out_shape=tuple(jax.ShapeDtypeStruct(*entry) for entry in POOLED),
        in_specs=[SMEM] + [VMEM] * 4 + [HBM] * (2 * SIDE),
        out_specs=(HBM,) * (2 * SIDE),
        scratch_shapes=POOL_SCRATCH + POOLED_SCRATCH,
        input_output_aliases={5 + place: place for place in range(2 * SIDE)},
        compiler_params=PARAMS,
        cost_estimate=pl.CostEstimate(flops=8 * 10**9, bytes_accessed=8 * 10**6, transcendentals=0),
        name="run_pool",
    )(counts, records, boxes, feature_map, table, *before)


def head_kernel(
    record_ref, box_ref, b1_ref, w2_ref, b2_ref, wp_ref, bp_ref, w1_ref, *refs
):
    parts, refs = refs[: 2 * SIDE], refs[2 * SIDE + 5 :]
    kept_out, next_ref, refs = refs[:5], refs[5], refs[6:]
    pooled_ref, pooled_sems, w1_buf, pre1, pre2, act1, act2, pred, w_sems, sems = refs

    @pl.when(lax.axis_index("section") == 1)
    def _():
        weight_copy(w1_ref, w1_buf, w_sems, 0).start()
        pooled_copies(pooled_ref, parts, pooled_sems, "in", True)
        weight_copy(w1_ref, w1_buf, w_sems, 1).start()

        def ready(piece):
            @pl.when(piece == 0)
            def _():
                pooled_copies(pooled_ref, parts, pooled_sems, "in", False)
                weight_copy(w1_ref, w1_buf, w_sems, 2).start()

            @pl.when(piece + 3 < PIECES)
            def _():
                weight_copy(w1_ref, w1_buf, w_sems, piece + 3).start()

        first_layer(pooled_ref, w1_ref, w1_buf, w_sems, b1_ref, pre1, ready)
        copies = [
            pltpu.make_async_copy(here, there, sems.at[place])
            for place, (here, there) in enumerate(zip((pre1, pre2, act1, act2, pred), kept_out))
        ]
        later_layers(
            1,
            own_records(record_ref, box_ref),
            pre1,
            pre2,
            act1,
            act2,
            pred,
            next_ref,
            w2_ref,
            b2_ref,
            wp_ref,
            bp_ref,
            lambda place: copies[place].start(),
        )
        for copy in copies:
            copy.wait()


def run_head(records, boxes, weights, parts, kept):
    return pl.pallas_call(
        head_kernel,
        out_shape=tuple(jax.ShapeDtypeStruct(*entry) for entry in KEPT)
        + (jax.ShapeDtypeStruct((SLOTS, 128), F32),),
        in_specs=[VMEM] * 7 + [HBM] * (1 + 2 * SIDE + 5),
        out_specs=(HBM,) * 5 + (VMEM,),
        scratch_shapes=POOLED_SCRATCH + HEAD_SCRATCH,
        input_output_aliases={8 + 2 * SIDE + place: place for place in range(5)},
        compiler_params=PARAMS,
        cost_estimate=pl.CostEstimate(
            flops=10**10, bytes_accessed=40 * 10**6, transcendentals=6 * 10**5
        ),
        name="run_head",
    )(records, boxes, *weights, *parts, *kept)


def put_parts(values, high_ref, low_ref):
    high = values.astype(BF16)
    high_ref[...] = high
    low_ref[...] = (values - high.astype(F32)).astype(BF16)


def put_tail(target, bias, boxes):
    target[:, 512:] = jnp.zeros((TAIL, target.shape[1] - 512), BF16)
    put_parts(bias, target.at[:, 0:256], target.at[:, 256:512])
    put_parts(boxes, target.at[:, 512:528], target.at[:, 528:544])


def pass_tail(target, bias, back_ref, own):
    target[:, 640:] = jnp.zeros((TAIL, target.shape[1] - 640), BF16)
    put_parts(bias, target.at[:, 0:256], target.at[:, 256:512])
    target[:, 512:640] = back_ref[pl.ds(own, 16, stride=SIDE), :].astype(BF16)


def take_tails(tails, back_ref):
    for k, tail in enumerate(tails):
        back_ref[k * 16 : (k + 1) * 16, :] = tail[:, 512:640].astype(F32)
    near, here, far, across = [
        tail[:, 0:256].astype(F32) + tail[:, 256:512].astype(F32) for tail in tails
    ]
    return (near + far) + (here + across)


def slope_kernel(
    record_ref,
    place_ref,
    next0_ref,
    next1_ref,
    pred,
    pre1,
    pre2,
    act1,
    act2,
    w2_ref,
    wp_ref,
    grad_ref,
    turned_ref,
    c0,
    c1,
    c2,
    c3,
    extra_ref,
    bias_ref,
    back_ref,
    sorted_ref,
):
    own_x, own_z, own_y = coordinates()
    first_section = lax.axis_index("section") == 0
    factor = jnp.where(first_section, 1.0, 0.5).astype(F32)
    records = record_ref[...]
    values = pred[...]
    lane = lax.broadcasted_iota(jnp.int32, values.shape, 1)
    is_class = lane < CLASSES
    peak = jnp.max(jnp.where(is_class, values, -jnp.inf), axis=1, keepdims=True)
    shares = jnp.where(is_class, jnp.exp(values - peak), 0.0)
    shares = shares / jnp.sum(shares, axis=1, keepdims=True)
    label = records[:, LABEL : LABEL + 1]
    weight = factor * records[:, LIVE : LIVE + 1]
    truth = jnp.where(lane.astype(F32) == label, 1.0, 0.0)
    aims = jnp.zeros_like(values)
    for k in range(4):
        aims = jnp.where(lane == CLASSES + k, records[:, TARGET + k : TARGET + k + 1], aims)
    pull = jnp.minimum(jnp.maximum(values - aims, -1.0), 1.0)
    pull = jnp.where(lane < PRED, pull, 0.0) * jnp.where(label > 0.0, 1.0, 0.0)
    out_grad = (jnp.where(is_class, shares - truth, pull) * weight).astype(BF16)
    pred_bias = jnp.sum(out_grad.astype(F32), axis=0, keepdims=True)
    second = jnp.dot(out_grad, wp_ref[...], preferred_element_type=F32)
    second = (second * gelu_slope(pre2[...])).astype(BF16)
    second_bias = jnp.sum(second.astype(F32), axis=0, keepdims=True)
    first = lax.dot_general(
        second, w2_ref[...], (((1,), (1,)), ((), ())), preferred_element_type=F32
    )
    first = (first * gelu_slope(pre1[...])).astype(BF16)
    grad_ref[...] = first
    wide = first.astype(F32)
    first_bias = jnp.sum(wide, axis=0, keepdims=True)
    turned = wide.T.astype(BF16)
    turned_ref[...] = turned
    second_turned = second.astype(F32).T.astype(BF16)
    extra_ref[:, :HIDDEN] = jnp.dot(
        second_turned, act1[...], preferred_element_type=F32
    ).astype(BF16)
    act2_turned = act2[...].astype(F32).T.astype(BF16)
    extra_ref[:, HIDDEN:] = jnp.dot(
        act2_turned, out_grad, preferred_element_type=F32
    ).astype(BF16)
    bias_ref[...] = jnp.zeros_like(bias_ref)
    for row in range(4):
        bias_ref[row : row + 1, :] = first_bias[:, row * 256 : (row + 1) * 256]
        bias_ref[4 + row : 5 + row, :] = second_bias[:, row * 256 : (row + 1) * 256]
    bias_ref[8:9, :128] = pred_bias
    order = jnp.where(
        lax.broadcasted_iota(jnp.int32, (SLOTS, SLOTS), 1).astype(F32) == place_ref[:, 0:1],
        1.0,
        0.0,
    )
    mine = jnp.where(first_section, next0_ref[...], next1_ref[...])
    boxes = jnp.dot(order, mine, precision=EXACT, preferred_element_type=F32)
    small_lane = lax.broadcasted_iota(jnp.int32, (GROUPS, 128), 1)
    back = jnp.zeros((GROUPS, 128), F32)
    for c in range(4):
        for k in range(4):
            back = jnp.where(
                small_lane == 4 * c + k, boxes[c * GROUPS : (c + 1) * GROUPS, k : k + 1], back
            )
    back_ref[...] = back
    for x in range(SIDE):
        for y in range(SIDE):
            sorted_ref[(x * SIDE + y) * SIDE : (x * SIDE + y + 1) * SIDE, :] = back_ref[
                pl.ds(x * 16 + y, SIDE, stride=SIDE), :
            ]
    for jx, target in enumerate((c0, c1, c2, c3)):
        for jz in range(SIDE):
            for jy in range(SIDE):
                source = (
                    (own_x + jx) % SIDE * 256 + (own_z + jz) % SIDE * 64 + (own_y + jy) % SIDE * 16
                )
                to = (jz * SIDE + jy) * 16
                target[to : to + 16, :] = extra_ref[pl.ds(pl.multiple_of(source, 16), 16), :]
        rows = pl.ds(pl.multiple_of((own_x + jx) % SIDE * 16, 16), 16)
        put_tail(target.at[256:, :], bias_ref[...], sorted_ref[rows, :16])


def run_slopes(records, places, after_first, after_second, kept, w2, wp):
    pre1, pre2, act1, act2, pred = kept
    return pl.pallas_call(
        slope_kernel,
        out_shape=(
            jax.ShapeDtypeStruct((SLOTS, HIDDEN), BF16),
            jax.ShapeDtypeStruct((HIDDEN, SLOTS), BF16),
        )
        + (jax.ShapeDtypeStruct((256 + TAIL, EXTRA), BF16),) * SIDE,
        in_specs=[VMEM] * 11,
        out_specs=(VMEM,) * 6,
        scratch_shapes=[
            pltpu.VMEM((HIDDEN, EXTRA), BF16),
            pltpu.VMEM((TAIL, 256), F32),
            pltpu.VMEM((GROUPS, 128), F32),
            pltpu.VMEM((GROUPS, 128), F32),
        ],
        compiler_params=PARAMS,
        cost_estimate=pl.CostEstimate(
            flops=10**6, bytes_accessed=10**5, transcendentals=0
        ),
        name="run_slopes",
    )(records, places, after_first, after_second, pred, pre1, pre2, act1, act2, w2, wp)


def pooled_grad_kernel(grad_ref, w1_ref, out_ref, w1_buf, out_buf, w_sems, out_sems):
    def out_copy(piece):
        columns = pl.ds(pl.multiple_of(piece * PIECE, PIECE), PIECE)
        return pltpu.make_async_copy(out_buf.at[piece], out_ref.at[:, columns], out_sems.at[piece])

    for piece in range(3):
        weight_copy(w1_ref, w1_buf, w_sems, piece).start()

    def one_piece(piece, carry):
        @pl.when(piece + 3 < PIECES)
        def _():
            weight_copy(w1_ref, w1_buf, w_sems, piece + 3).start()

        weight_copy(w1_ref, w1_buf, w_sems, piece).wait()
        rows = pl.ds(pl.multiple_of(piece * PIECE, PIECE), PIECE)
        out_buf[piece] = lax.dot_general(
            grad_ref[...], w1_buf[rows, :], (((1,), (1,)), ((), ())), preferred_element_type=F32
        ).astype(BF16)
        out_copy(piece).start()
        return carry

    lax.fori_loop(0, PIECES, one_piece, 0)

    def finish(piece, carry):
        out_copy(piece).wait()
        return carry

    lax.fori_loop(0, PIECES, finish, 0)


def run_pooled_grad(grad, w1):
    return pl.pallas_call(
        pooled_grad_kernel,
        out_shape=jax.ShapeDtypeStruct((SLOTS, FEATURES), BF16),
        in_specs=[VMEM, HBM],
        out_specs=HBM,
        scratch_shapes=[
            pltpu.VMEM((FEATURES, HIDDEN), BF16),
            pltpu.VMEM((PIECES, SLOTS, PIECE), BF16),
            pltpu.SemaphoreType.DMA((PIECES,)),
            pltpu.SemaphoreType.DMA((PIECES,)),
        ],
        compiler_params=PARAMS,
        cost_estimate=pl.CostEstimate(
            flops=2 * SLOTS * FEATURES * HIDDEN, bytes_accessed=33 * 10**6, transcendentals=0
        ),
        name="run_pooled_grad",
    )(grad, w1)


def scatter_kernel(
    count_ref,
    record_ref,
    box_ref,
    table_ref,
    grad_ref,
    out_ref,
    coord_ref,
    spread_ref,
    turned_ref,
    rows_ref,
    grad_buf,
    slot_ref,
    wide_ref,
    sems,
):
    up_to = [count_ref[octave] for octave in range(4)]
    lane = lax.broadcasted_iota(jnp.int32, (1, 128), 1)
    lane_bin = lane // GROUP

    def grad_copy(quarter):
        rows = pl.ds(pl.multiple_of(quarter * SLOT_QUARTER, SLOT_QUARTER), SLOT_QUARTER)
        return pltpu.make_async_copy(grad_ref.at[rows, :], grad_buf.at[rows, :], sems.at[quarter])

    for quarter in range(SIDE):
        grad_copy(quarter).start()
    out_ref[...] = jnp.zeros_like(out_ref)
    rows_ref[...] = jnp.zeros_like(rows_ref)
    records = record_ref[...]
    wide_lane = lax.broadcasted_iota(jnp.int32, records.shape, 1)
    passed = (wide_lane < 4) & (lax.axis_index("section") == 1)
    records = jnp.where(passed, box_ref[...], records)
    coords = sample_coordinates(records)
    coords = jnp.where(wide_lane == 32, records[:, LEVEL : LEVEL + 1], coords)
    slot_ref[...] = coords
    left = coords.T[:48, :]
    repeat = jnp.where(
        lax.broadcasted_iota(jnp.int32, (SLOTS, 2048), 0)
        == lax.broadcasted_iota(jnp.int32, (SLOTS, 2048), 1) // 128 * GROUP
        + lax.broadcasted_iota(jnp.int32, (SLOTS, 2048), 1) % GROUP,
        1.0,
        0.0,
    ).astype(BF16)
    wide = jnp.zeros((48, 2048), F32)
    for _ in range(3):
        part = left.astype(BF16)
        left = left - part.astype(F32)
        wide = wide + jnp.dot(part, repeat, preferred_element_type=F32)
    wide_ref[...] = wide

    def one_quarter(quarter, carry):
        grad_copy(quarter).wait()
        first = quarter * (SLOT_QUARTER // GROUP)
        live = (up_to[3] + GROUP - 1) // GROUP
        lax.fori_loop(first, jnp.minimum(first + SLOT_QUARTER // GROUP, live), one_group, 0)
        return carry

    def one_group(group, carry):
        start = pl.multiple_of(group * GROUP, GROUP)
        coords = slot_ref[pl.ds(start, GROUP), :]
        coord_ref[...] = wide_ref[:, pl.ds(pl.multiple_of(group * 128, 128), 128)]
        for p in range(7):
            for q in range(7):
                spot = p * 7 + q
                rows_ref[p * 128 + q * GROUP : p * 128 + (q + 1) * GROUP, :] = grad_buf[
                    pl.ds(start, GROUP), spot * CHANNELS : (spot + 1) * CHANNELS
                ]

        def column_ends():
            ends = []
            for side in range(2):
                value = jnp.full((1, 128), -2000.0, F32)
                for q in range(7):
                    row = 16 + 2 * q + side
                    value = jnp.where(lane_bin == q, coord_ref[row : row + 1, :], value)
                ends.append(value)
            return ends

        def ends_of_row(p):
            return coord_ref[2 * p : 2 * p + 1, :], coord_ref[2 * p + 1 : 2 * p + 2, :]

        def grid_block(height, first_row):
            width = 48
            left, right = column_ends()
            wanted = coord_ref[32:33, :] == 0.0
            x_cells = 0.5 * lax.broadcasted_iota(jnp.int32, (width, 128), 0).astype(F32)
            y_cells = 0.5 * (
                lax.broadcasted_iota(jnp.int32, (height, 128), 0) + first_row
            ).astype(F32)
            columns = jnp.where(wanted, tent_pair(left, right, x_cells), 0.0)
            cells = height * width
            for p in range(7):
                top, bottom = ends_of_row(p)
                spread_ref[:height, :] = tent_pair(top, bottom, y_cells)
                for y in range(height):
                    turned_ref[y * width : (y + 1) * width, p * 128 : (p + 1) * 128] = (
                        spread_ref[y : y + 1, :] * columns
                    ).astype(BF16)
            out_ref[pl.ds(pl.multiple_of(first_row * 48, 16), cells), :] += jnp.dot(
                turned_ref[:cells, :], rows_ref[...], preferred_element_type=F32
            )

        @pl.when(start < up_to[0])
        def _():
            first, count = row_window(coords, coords[:, 32:33] == 0.0)

            @pl.when(count <= 10)
            def _():
                grid_block(10, jnp.minimum(first, 22))

            @pl.when((count > 10) & (count <= 20))
            def _():
                grid_block(20, jnp.minimum(first, 12))

            @pl.when(count > 20)
            def _():
                grid_block(32, jnp.int32(0))

        @pl.when((start + GROUP > up_to[0]) & (start < up_to[1]))
        def _():
            left, right = column_ends()
            wanted = coord_ref[32:33, :] == 1.0
            x_cells = 0.5 * lax.broadcasted_iota(jnp.int32, (24, 128), 0).astype(F32)
            y_cells = 0.5 * lax.broadcasted_iota(jnp.int32, (16, 128), 0).astype(F32)
            columns = jnp.where(wanted, tent_pair(left, right, x_cells), 0.0)
            for p in range(7):
                top, bottom = ends_of_row(p)
                spread_ref[:16, :] = tent_pair(top, bottom, y_cells)
                for y in range(0, 16, 2):
                    both = jnp.concatenate(
                        [spread_ref[y : y + 1, :] * columns, spread_ref[y + 1 : y + 2, :] * columns],
                        axis=0,
                    )
                    turned_ref[y * 24 : (y + 2) * 24, p * 128 : (p + 1) * 128] = both.astype(BF16)
            out_ref[1536:1920, :] += jnp.dot(
                turned_ref[:384, :], rows_ref[...], preferred_element_type=F32
            )

        @pl.when((start + GROUP > up_to[1]) & (start < up_to[3]))
        def _():
            left, right = column_ends()
            y_cells = table_ref[:, 0:1]
            x_cells = table_ref[:, 1:2]
            wanted = coord_ref[32:33, :] == table_ref[:, 2:3]
            columns = jnp.where(wanted, tent_pair(left, right, x_cells), 0.0)
            for p in range(7):
                top, bottom = ends_of_row(p)
                turned_ref[:128, p * 128 : (p + 1) * 128] = (
                    tent_pair(top, bottom, y_cells) * columns
                ).astype(BF16)
            update = jnp.dot(turned_ref[:128, :], rows_ref[...], preferred_element_type=F32)
            out_ref[1920:CELLS, :] += update[: CELLS - 1920, :]

        return carry

    lax.fori_loop(0, SIDE, one_quarter, 0)


def run_scatter(counts, records, boxes, table, pooled_grad):
    return pl.pallas_call(
        scatter_kernel,
        out_shape=jax.ShapeDtypeStruct((CELLS, CHANNELS), F32),
        in_specs=[SMEM, VMEM, VMEM, VMEM, HBM],
        out_specs=VMEM,
        scratch_shapes=[
            pltpu.VMEM((48, 128), F32),
            pltpu.VMEM((32, 128), F32),
            pltpu.VMEM((1536, 7 * 128), BF16),
            pltpu.VMEM((7 * 128, CHANNELS), BF16),
            pltpu.VMEM((SLOTS, FEATURES), BF16),
            pltpu.VMEM((SLOTS, 128), F32),
            pltpu.VMEM((48, 2048), F32),
            pltpu.SemaphoreType.DMA((SIDE,)),
        ],
        compiler_params=PARAMS,
        cost_estimate=pl.CostEstimate(
            flops=2 * 10**10, bytes_accessed=9 * 10**6, transcendentals=0
        ),
        name="run_scatter",
    )(counts, records, boxes, table, pooled_grad)


def load_pieces(turned_in, gained, pooled, turned, right, sems, piece_sems, steps):
    sources = [turned_in, *gained]
    first = [
        pltpu.make_async_copy(source, turned.at[k], sems.at[k]) for k, source in enumerate(sources)
    ]
    later = [
        [
            pltpu.make_async_copy(
                pooled[k].at[:, start : start + width],
                right.at[pl.ds(k * SLOTS, SLOTS), start : start + width],
                piece_sems.at[step, k],
            )
            for k in range(SIDE)
        ]
        for step, (start, width) in enumerate(steps)
    ]
    for copy in first:
        copy.start()
    for copies in later:
        for copy in copies:
            copy.start()
    return first, later


def place_left(left, turned, row_of):
    own_x, own_z, own_y = coordinates()
    for j in range(SIDE):
        for i in range(SIDE):
            for h in range(SIDE):
                jx, jz, jy = row_of(j, i, h)
                source = (
                    (own_x + jx) % SIDE * 256 + (own_z + jz) % SIDE * 64 + (own_y + jy) % SIDE * 16
                )
                to = ((j * SIDE + i) * SIDE + h) * 16
                for k in range(SIDE):
                    left[to : to + 16, k * SLOTS : (k + 1) * SLOTS] = turned[
                        k, pl.ds(pl.multiple_of(source, 16), 16), :
                    ]


def multiply(left, right, part, start, width):
    def one(step, carry):
        columns = pl.ds(pl.multiple_of(start + step * 256, 128), 256)
        value = jnp.dot(left[...], right[:, columns], preferred_element_type=F32).astype(BF16)
        for j in range(SIDE):
            part[j, :256, columns] = value[j * 256 : (j + 1) * 256, :]
        return carry

    lax.fori_loop(0, width // 256, one, 0)
    if width % 256:
        end = start + width
        value = jnp.dot(
            left[...], right[:, end - 128 : end], preferred_element_type=F32
        ).astype(BF16)
        for j in range(SIDE):
            part[j, :256, end - 128 : end] = value[j * 256 : (j + 1) * 256, :]


STEPS_Y = ((0, 512), (512, 768))
STEPS_Z = ((0, 768), (768, 1152))


def weight_grad_kernel(steps, row_of, extra_count, *refs):
    turned_in, gained, pooled = refs[0], refs[1:4], refs[4:8]
    extras, refs = refs[8 : 8 + extra_count], refs[8 + extra_count :]
    outs, (turned, right, left, part, sems, piece_sems, out_sems) = refs[:SIDE], refs[SIDE:]
    added = [
        pltpu.make_async_copy(extra, part.at[j, :, PART_Y:], out_sems.at[SIDE + j])
        for j, extra in enumerate(extras)
    ]
    for copy in added:
        copy.start()
    first, later = load_pieces(turned_in, gained, pooled, turned, right, sems, piece_sems, steps)
    for copy in first:
        copy.wait()
    place_left(left, turned, row_of)
    for copies, (start, width) in zip(later, steps):
        for copy in copies:
            copy.wait()
        multiply(left, right, part, start, width)
    for copy in added:
        copy.wait()
    results = [pltpu.make_async_copy(part.at[j], outs[j], out_sems.at[j]) for j in range(SIDE)]
    for copy in results:
        copy.start()
    for copy in results:
        copy.wait()


def run_weight_grad(name, steps, row_of, turned, gained, pooled, extra=()):
    width = pooled[0].shape[1]
    shape = (256 + TAIL, width + EXTRA) if extra else (256, width)
    return pl.pallas_call(
        lambda *refs: weight_grad_kernel(steps, row_of, len(extra), *refs),
        out_shape=(jax.ShapeDtypeStruct(shape, BF16),) * SIDE,
        in_specs=[HBM] * (8 + len(extra)),
        out_specs=(HBM,) * SIDE,
        scratch_shapes=[
            pltpu.VMEM((SIDE, HIDDEN, SLOTS), BF16),
            pltpu.VMEM((HIDDEN, width), BF16),
            pltpu.VMEM((HIDDEN, HIDDEN), BF16),
            pltpu.VMEM((SIDE, *shape), BF16),
            pltpu.SemaphoreType.DMA((SIDE,)),
            pltpu.SemaphoreType.DMA((len(steps), SIDE)),
            pltpu.SemaphoreType.DMA((2 * SIDE,)),
        ],
        compiler_params=PARAMS,
        cost_estimate=pl.CostEstimate(
            flops=3 * HIDDEN * HIDDEN * width, bytes_accessed=9 * 10**6, transcendentals=0
        ),
        name=name,
    )(turned, *gained, *pooled, *extra)


def add_rows(ins, rows):
    total = ins[0][rows, :].astype(F32)
    for k in range(1, SIDE):
        total += ins[k][rows, :].astype(F32)
    return total


def sum_y_first_kernel(*refs):
    ins, outs, back_ref = refs[:SIDE], refs[SIDE : 2 * SIDE], refs[2 * SIDE]
    own_x, own_z, own_y = coordinates()
    bias = take_tails([part.at[256:, PART_Y:] for part in ins], back_ref)
    for j in range(SIDE):
        outs[j][:64, :] = add_rows(ins, slice(64 * j, 64 * (j + 1))).astype(BF16)
        outs[j][64:, :PART_Y] = jnp.zeros((TAIL, PART_Y), BF16)
        pass_tail(outs[j].at[64:, PART_Y:], bias, back_ref, (own_z + j) % SIDE)


def sum_y_first(parts):
    return pl.pallas_call(
        sum_y_first_kernel,
        out_shape=(jax.ShapeDtypeStruct((64 + TAIL, WIDE_Y), BF16),) * SIDE,
        in_specs=[VMEM] * SIDE,
        out_specs=(VMEM,) * SIDE,
        scratch_shapes=[pltpu.VMEM((GROUPS, 128), F32)],
        compiler_params=SMALL,
        cost_estimate=pl.CostEstimate(flops=10**6, bytes_accessed=4 * 10**6, transcendentals=0),
        name="sum_y_first",
    )(*parts)


def sum_y_second_kernel(*refs):
    ins, outs, back_ref = refs[:SIDE], refs[SIDE : 2 * SIDE], refs[2 * SIDE]
    own_x, own_z, own_y = coordinates()
    bias = take_tails([part.at[64:, PART_Y:] for part in ins], back_ref)
    for j in range(SIDE):
        outs[j][:16, :] = add_rows(ins, slice(16 * j, 16 * (j + 1))).astype(BF16)
        outs[j][16:, :PART_Y] = jnp.zeros((TAIL, PART_Y), BF16)
        pass_tail(outs[j].at[16:, PART_Y:], bias, back_ref, (own_y + j) % SIDE)


def sum_y_second(parts):
    return pl.pallas_call(
        sum_y_second_kernel,
        out_shape=(jax.ShapeDtypeStruct((16 + TAIL, WIDE_Y), BF16),) * SIDE,
        in_specs=[VMEM] * SIDE,
        out_specs=(VMEM,) * SIDE,
        scratch_shapes=[pltpu.VMEM((GROUPS, 128), F32)],
        compiler_params=SMALL,
        cost_estimate=pl.CostEstimate(flops=10**6, bytes_accessed=10**6, transcendentals=0),
        name="sum_y_second",
    )(*parts)


def sum_z_kernel(rows, *refs):
    ins, outs = refs[:SIDE], refs[SIDE:]
    for j in range(SIDE):
        outs[j][...] = add_rows(ins, slice(rows * j, rows * (j + 1))).astype(BF16)


def sum_z(parts):
    rows = parts[0].shape[0] // SIDE
    return pl.pallas_call(
        lambda *refs: sum_z_kernel(rows, *refs),
        out_shape=(jax.ShapeDtypeStruct((rows, PART_Z), BF16),) * SIDE,
        in_specs=[VMEM] * SIDE,
        out_specs=(VMEM,) * SIDE,
        compiler_params=SMALL,
        cost_estimate=pl.CostEstimate(flops=10**6, bytes_accessed=10**6, transcendentals=0),
        name="sum_z",
    )(*parts)


def join_kernel(image_ref, *refs):
    parts_y, parts_z = refs[:SIDE], refs[SIDE : 2 * SIDE]
    out_ref, second_ref, pred_ref, first_bias, second_bias, pred_bias, refined_ref = refs[
        2 * SIDE : 2 * SIDE + 7
    ]
    back_ref, bias_ref = refs[2 * SIDE + 7 :]
    own_x, own_z, own_y = coordinates()
    for parts, own, width, first in (
        (parts_y, own_y, PART_Y, 0),
        (parts_z, own_z, PART_Z, SPLIT),
    ):
        for k in range(SIDE):
            for chunk in range(SIDE):
                start = first + chunk * width
                count = min(width, FEATURES - start)

                @pl.when((own - k + SIDE) % SIDE == chunk)
                def _():
                    out_ref[:, start : start + count] = parts[k][:16, :count].astype(F32)

    extra = [part.at[:, PART_Y:] for part in parts_y]
    total = add_rows(extra, slice(0, 16))
    second_ref[...] = total[:, :HIDDEN]
    pred_ref[...] = total[:, HIDDEN:]
    bias_ref[...] = take_tails([part.at[16:, :] for part in extra], back_ref)
    for row in range(4):
        lanes = slice(row * 256, (row + 1) * 256)
        first_bias[:, lanes] = bias_ref[row : row + 1, :]
        second_bias[:, lanes] = bias_ref[4 + row : 5 + row, :]
    pred_bias[...] = bias_ref[8:9, :128]
    images = image_ref[...]
    slot = slot_of_regions(images.astype(F32))
    owner = (
        jnp.bitwise_and(own_y - images, 3) * 16
        + jnp.bitwise_and(own_z - (images >> 2), 3) * 4
        + jnp.bitwise_and(own_x - (images >> 4), 3)
    )
    chosen = jnp.where(lax.broadcasted_iota(jnp.int32, (GROUPS, REGIONS), 0) == owner, 1.0, 0.0)
    values = jnp.dot(back_ref[...].T, chosen, precision=EXACT, preferred_element_type=F32)
    values = values[:16, :] + values[16:32, :]
    result = jnp.zeros((4, REGIONS), F32)
    for c in range(4):
        result = jnp.where(slot == float(c), values[4 * c : 4 * c + 4, :], result)
    refined_ref[...] = result


def join_parts(images, parts_y, parts_z):
    return pl.pallas_call(
        join_kernel,
        out_shape=(
            jax.ShapeDtypeStruct((16, FEATURES), F32),
            jax.ShapeDtypeStruct((16, HIDDEN), F32),
            jax.ShapeDtypeStruct((16, 128), F32),
            jax.ShapeDtypeStruct((1, HIDDEN), F32),
            jax.ShapeDtypeStruct((1, HIDDEN), F32),
            jax.ShapeDtypeStruct((1, 128), F32),
            jax.ShapeDtypeStruct((4, REGIONS), F32),
        ),
        in_specs=[VMEM] * (1 + 2 * SIDE),
        out_specs=(VMEM,) * 7,
        scratch_shapes=[pltpu.VMEM((GROUPS, 128), F32), pltpu.VMEM((TAIL, 256), F32)],
        compiler_params=SMALL,
        cost_estimate=pl.CostEstimate(flops=10**6, bytes_accessed=2 * 10**6, transcendentals=0),
        name="join_parts",
    )(images, *parts_y, *parts_z)


def ring(arrays, axis):
    return [arrays[0]] + [shift(arrays[by], axis, by) for by in range(1, SIDE)]


def body(
    pyramid,
    boxes,
    image_ids,
    levels,
    labels,
    targets,
    w_first,
    b_first,
    w_second,
    b_second,
    w_pred,
    b_pred,
):
    rows, cols, cell_levels = cell_tables()
    lane_table = jnp.asarray(np.stack([rows, cols, cell_levels] + [np.zeros_like(rows)] * 5))
    side_table = np.zeros((128, 128), np.float32)
    side_table[:, 0], side_table[:, 1], side_table[:, 2] = (
        rows[1920:],
        cols[1920:],
        cell_levels[1920:],
    )
    side_table = jnp.asarray(side_table)
    feature_map = jnp.pad(pyramid[0], ((0, CELLS_PAD - CELLS), (0, 0)))
    pred_weight = jnp.pad(w_pred[0], ((0, 128 - PRED), (0, 0)))
    pred_bias = jnp.pad(b_pred, ((0, 0), (0, 128 - PRED)))
    image_row = image_ids.reshape(1, REGIONS)

    with jax.named_scope("regions_to_images"):
        sent = send_regions(image_row, boxes, levels.reshape(1, REGIONS), labels, targets[0])
        got = lax.all_to_all(sent, "region", 0, 0, tiled=True)
    records, places, counts = select_slots(got)
    weights = (b_first, w_second[0], b_second, pred_weight, pred_bias, w_first[0])

    *kept, after_first = run_forward(counts, records, feature_map, lane_table, weights)
    with jax.named_scope("boxes_to_second"):
        passed = lax.ppermute(after_first, "section", [(0, 1)])
    kept, pooled = kept[2 * SIDE :], kept[: 2 * SIDE]
    pooled = run_pool(counts, records, passed, feature_map, lane_table, pooled)
    with jax.named_scope("pooled_over_rings"):
        pooled_y = ring(pooled[:SIDE], "y")
        pooled_z = [pooled[SIDE]] + [shift(pooled[SIDE + by], "z", by) for by in (1, 3)]
    *kept, after_second = run_head(records, passed, weights, pooled, kept)
    last, kept[0] = lax.optimization_barrier((pooled[SIDE + 2], kept[0]))
    with jax.named_scope("pooled_over_rings"):
        pooled_z.insert(2, shift(last, "z", 2))
    grad, turned, *extra = run_slopes(
        records, places, after_first, after_second, kept, w_second[0], pred_weight
    )
    *joined, grad = lax.optimization_barrier((*pooled_y, *pooled_z, grad))
    pooled_y, pooled_z = joined[:SIDE], joined[SIDE:]
    with jax.named_scope("gradient_over_rings"):
        gained_y = ring([turned] * SIDE, "y")[1:]
        gained_z = [shift(turned, "z", by) for by in (1, 3)]
    pooled_grad = run_pooled_grad(grad, w_first[0])
    *gained_z, pooled_grad, turned = lax.optimization_barrier((*gained_z, pooled_grad, turned))
    with jax.named_scope("gradient_over_rings"):
        gained_z.insert(1, shift(turned, "z", 2))
    part_y = run_weight_grad(
        "run_grad_y", STEPS_Y, lambda j, i, h: (j, i, h), turned, gained_y, pooled_y, extra
    )
    *part_y, turned = lax.optimization_barrier((*part_y, turned))
    part_z = run_weight_grad(
        "run_grad_z", STEPS_Z, lambda j, i, h: (i, h, j), turned, gained_z, pooled_z
    )
    *part_z, pooled_grad = lax.optimization_barrier((*part_z, pooled_grad))
    map_grad = run_scatter(counts, records, passed, side_table, pooled_grad)
    with jax.named_scope("sum_over_rings"):
        part_y, part_z = ring(part_y, "x"), ring(part_z, "y")
        part_y[0], part_z[0], map_grad = lax.optimization_barrier((part_y[0], part_z[0], map_grad))
        part_y = ring(sum_y_first(part_y), "z")
        part_z = ring(sum_z(part_z), "x")
        part_y, part_z = sum_y_second(part_y), sum_z(part_z)
    with jax.named_scope("columns_over_rings"):
        first, second, pred, first_bias, second_bias, bias, refined = join_parts(
            image_row, ring(part_y, "y"), ring(part_z, "z")
        )
    return (
        first.T[None],
        first_bias,
        second.T[None],
        second_bias,
        pred[:, :PRED].T[None],
        bias[:, :PRED],
        map_grad[None, None],
        refined[None],
    )


def solution(mesh):
    return jax.shard_map(
        body,
        mesh=mesh,
        in_specs=(
            P("region", None, None),
            P(None, "region"),
            P("region", None),
            P("region"),
            P("section", "region"),
            P("section", None, "region"),
            P("section", None, None),
            P("section", None),
            P("section", None, None),
            P("section", None),
            P("section", None, None),
            P("section", None),
        ),
        out_specs=(
            P("section", None, "region"),
            P("section", None),
            P("section", None, "region"),
            P("section", None),
            P("section", None, "region"),
            P("section", None),
            P("section", "region", None, None),
            P("section", None, "region"),
        ),
        check_vma=False,
    )
```

```python
import jax
import jax.numpy as jnp
import numpy as np
from jax import lax
from jax.experimental import pallas as pl
from jax.experimental.pallas import tpu as pltpu
from jax.sharding import PartitionSpec as P

SIDE = 4
GROUPS = 64
SLOTS = 256
GROUP = 16
SLOT_QUARTER = 64
REGIONS = 128
CHANNELS = 256
BINS = 49
FEATURES = 12544
HIDDEN = 1024
CLASSES = 81
PRED = 85
PART_Y = 1024
PART_Z = 2176
SPLIT = SIDE * PART_Y
WIDE = SPLIT + SIDE * PART_Z
EXTRA = HIDDEN + 128
TAIL = 16
WIDE_Y = PART_Y + EXTRA
CELLS = 2040
CELLS_PAD = 2048
EXACT = lax.Precision.HIGHEST
F32 = jnp.float32
BF16 = jnp.bfloat16
HBM = pl.BlockSpec(memory_space=pltpu.HBM)
VMEM = pl.BlockSpec(memory_space=pltpu.VMEM)
SMEM = pl.BlockSpec(memory_space=pltpu.SMEM)
MIB = 1 << 20
PARAMS = pltpu.CompilerParams(vmem_limit_bytes=60 * MIB)
SMALL = pltpu.CompilerParams(vmem_limit_bytes=16 * MIB)

BOX, LEVEL, LABEL, TARGET, LIVE = 0, 4, 5, 6, 10
FIELDS = 16


def ring_pairs(axis, by):
    step = {"x": 16, "z": 4, "y": 1}[axis]
    pairs = []
    for source in range(GROUPS):
        place = source // step % SIDE
        pairs.append((source, source + ((place + by) % SIDE - place) * step))
    return pairs


def shift(array, axis, by):
    return lax.ppermute(array, "region", ring_pairs(axis, by))


def coordinates():
    own = lax.axis_index("region")
    return own // 16, own // 4 % SIDE, own % SIDE


def cell_tables():
    rows = np.full((CELLS_PAD,), -1000.0, np.float32)
    cols = np.full((CELLS_PAD,), -1000.0, np.float32)
    levels = np.full((CELLS_PAD,), -1.0, np.float32)
    start = 0
    for octave in range(4):
        height, width = 32 >> octave, 48 >> octave
        spots = np.arange(height * width)
        rows[start : start + height * width] = 0.5 * (spots // width)
        cols[start : start + height * width] = 0.5 * (spots % width)
        levels[start : start + height * width] = octave
        start += height * width
    return rows, cols, levels


def tent_pair(first, second, cells):
    return jnp.maximum(0.5 - jnp.abs(first - cells), 0.0) + jnp.maximum(
        0.5 - jnp.abs(second - cells), 0.0
    )


def sample_coordinates(records):
    lane = lax.broadcasted_iota(jnp.int32, records.shape, 1)
    level = records[:, LEVEL : LEVEL + 1]

    def of_level(values):
        return jnp.where(
            level == 0.0,
            values[0],
            jnp.where(level == 1.0, values[1], jnp.where(level == 2.0, values[2], values[3])),
        ).astype(F32)

    scale = of_level((0.25, 0.125, 0.0625, 0.03125))
    anchors, bins = [], []
    for low in (1, 0):
        lower, upper = records[:, low : low + 1], records[:, low + 2 : low + 3]
        anchors.append(lower * scale - 0.5)
        bins.append((upper - lower) * scale / 7.0)
    along_y = lane < 16
    offset = (jnp.where(along_y, lane, lane - 16).astype(F32) + 0.5) * 0.5
    coords = jnp.where(along_y, anchors[0], anchors[1]) + jnp.where(along_y, bins[0], bins[1]) * offset
    limit = jnp.where(along_y, of_level((31.0, 15.0, 7.0, 3.0)), of_level((47.0, 23.0, 11.0, 5.0)))
    return 0.5 * jnp.minimum(jnp.maximum(coords, 0.0), limit)


def row_window(coords, wanted):
    lane = lax.broadcasted_iota(jnp.int32, coords.shape, 1)
    mine = wanted & (lane < 14)
    low = jnp.min(jnp.where(mine, coords, 1000.0))
    high = jnp.max(jnp.where(mine, coords, -1000.0))
    first = (2.0 * low).astype(jnp.int32)
    return first, (2.0 * high).astype(jnp.int32) + 2 - first


def slot_of_regions(images):
    lane = lax.broadcasted_iota(jnp.int32, (1, REGIONS), 1)
    wide = jnp.broadcast_to(images, (REGIONS, REGIONS))
    row = lax.broadcasted_iota(jnp.int32, (REGIONS, REGIONS), 0)
    column = lax.broadcasted_iota(jnp.int32, (REGIONS, REGIONS), 1)
    earlier = (wide.T == wide) & (row < column) & ((row >= 64) == (column >= 64))
    second = jnp.max(jnp.where(earlier, 1.0, 0.0), axis=0, keepdims=True)
    return jnp.where(lane >= 64, 2.0, 0.0) + second


def send_kernel(image_ref, box_ref, level_ref, label_ref, target_ref, out_ref):
    images = image_ref[...].astype(F32)
    slots = slot_of_regions(images)
    fields = jnp.concatenate(
        [
            box_ref[...],
            level_ref[...].astype(F32),
            label_ref[...].astype(F32),
            target_ref[...],
            jnp.ones((1, REGIONS), F32),
            jnp.zeros((5, REGIONS), F32),
        ],
        axis=0,
    )
    owner = lax.broadcasted_iota(jnp.int32, (GROUPS, REGIONS), 0).astype(F32) == images
    out_ref[...] = jnp.zeros_like(out_ref)
    for c in range(4):
        chosen = jnp.where(owner & (slots == float(c)), 1.0, 0.0)
        out_ref[:, c * FIELDS : (c + 1) * FIELDS] = lax.dot_general(
            chosen, fields, (((1,), (1,)), ((), ())), precision=EXACT, preferred_element_type=F32
        )


def send_regions(images, boxes, levels, labels, targets):
    return pl.pallas_call(
        send_kernel,
        out_shape=jax.ShapeDtypeStruct((GROUPS, 128), F32),
        in_specs=[VMEM] * 5,
        out_specs=VMEM,
        compiler_params=SMALL,
        cost_estimate=pl.CostEstimate(flops=10**7, bytes_accessed=10**5, transcendentals=0),
        name="send_regions",
    )(images, boxes, levels, labels, targets)


def select_kernel(got_ref, record_ref, place_ref, count_ref, raw_ref):
    raw_ref[...] = jnp.zeros_like(raw_ref)
    for c in range(4):
        raw_ref[c * GROUPS : (c + 1) * GROUPS, :FIELDS] = got_ref[
            :, c * FIELDS : (c + 1) * FIELDS
        ]
    raw = raw_ref[...]
    lane = lax.broadcasted_iota(jnp.int32, (SLOTS, 128), 1)
    raw = jnp.where((lane == LEVEL) & (raw[:, LIVE : LIVE + 1] == 0.0), 4.0, raw)
    turned = raw.T
    spot_col = lax.broadcasted_iota(jnp.int32, (SLOTS, 1), 0).astype(F32)
    spot_row = lax.broadcasted_iota(jnp.int32, (1, SLOTS), 1).astype(F32)
    levels_row = turned[LEVEL : LEVEL + 1, :]
    key_col = raw[:, LEVEL : LEVEL + 1] * 1024.0 + raw[:, 1:2] + raw[:, 3:4]
    key_row = levels_row * 1024.0 + turned[1:2, :] + turned[3:4, :]
    same = key_col == key_row
    col_first = (key_col < key_row) | (same & (spot_col < spot_row))
    row_first = (key_row < key_col) | (same & (spot_row < spot_col))
    place_row = jnp.sum(jnp.where(col_first, 1.0, 0.0), axis=0, keepdims=True)
    place_col = jnp.sum(jnp.where(row_first, 1.0, 0.0), axis=1, keepdims=True)
    order = jnp.where(
        lax.broadcasted_iota(jnp.int32, (SLOTS, SLOTS), 0).astype(F32) == place_row, 1.0, 0.0
    )
    record_ref[...] = jnp.dot(order, raw, precision=EXACT, preferred_element_type=F32)
    place_ref[...] = jnp.broadcast_to(place_col, (SLOTS, 128))
    for octave in range(4):
        count_ref[octave] = jnp.sum(jnp.where(levels_row <= float(octave), 1, 0))


def select_slots(got):
    return pl.pallas_call(
        select_kernel,
        out_shape=(
            jax.ShapeDtypeStruct((SLOTS, 128), F32),
            jax.ShapeDtypeStruct((SLOTS, 128), F32),
            jax.ShapeDtypeStruct((8,), jnp.int32),
        ),
        in_specs=[VMEM],
        out_specs=(VMEM, VMEM, SMEM),
        scratch_shapes=[pltpu.VMEM((SLOTS, 128), F32)],
        compiler_params=SMALL,
        cost_estimate=pl.CostEstimate(flops=10**8, bytes_accessed=10**6, transcendentals=0),
        name="select_slots",
    )(got)


def gelu(values):
    inner = 0.7978845608028654 * (values + 0.044715 * (values * values * values))
    return 0.5 * values * (1.0 + jnp.tanh(inner))


def gelu_slope(values):
    square = values * values
    inner = 0.7978845608028654 * values * (1.0 + 0.044715 * square)
    bend = jnp.tanh(inner)
    slope = 0.7978845608028654 * (1.0 + 3.0 * 0.044715 * square)
    return 0.5 * (1.0 + bend) + 0.5 * values * (1.0 - bend * bend) * slope


PIECE = 1792
PIECES = FEATURES // PIECE


def pool_all(
    count_ref, records, map_ref, table_ref, coord_ref, level_ref, weight_ref, pooled_ref, send
):
    def level_block(rows, first_cell, cells, period, coords, wanted, first_row=None, begun=None):
        map_rows = slice(first_cell, first_cell + cells)
        if first_row is not None:
            map_rows = pl.ds(pl.multiple_of(first_row * 48, 16), cells)
            lane = lax.broadcasted_iota(jnp.int32, coords.shape, 1)
            coords = jnp.where(lane < 16, coords - 0.5 * first_row.astype(F32), coords)
        row_cells = table_ref[0:1, first_cell : first_cell + cells]
        col_cells = table_ref[1:2, first_cell : first_cell + period]
        columns = []
        for q in range(7):
            share = tent_pair(
                coords[:, 16 + 2 * q : 17 + 2 * q], coords[:, 17 + 2 * q : 18 + 2 * q], col_cells
            )
            columns.append(jnp.where(wanted, share, 0.0).astype(BF16))
        for p in range(7):
            share = tent_pair(
                coords[:, 2 * p : 2 * p + 1], coords[:, 2 * p + 1 : 2 * p + 2], row_cells
            ).astype(BF16)
            for q in range(7):
                for part in range(cells // period):
                    weight_ref[
                        (p * 7 + q) * GROUP : (p * 7 + q + 1) * GROUP,
                        part * period : (part + 1) * period,
                    ] = share[:, part * period : (part + 1) * period] * columns[q]
        total = jnp.dot(
            weight_ref[:, :cells], map_ref[map_rows, :], preferred_element_type=F32
        )
        for spot in range(BINS):
            value = total[spot * GROUP : (spot + 1) * GROUP, :]
            place = (rows, slice(spot * CHANNELS, (spot + 1) * CHANNELS))
            if begun is not None:
                value = value + jnp.where(begun, pooled_ref[place].astype(F32), 0.0)
            pooled_ref[place] = value.astype(BF16)

    coord_ref[...] = sample_coordinates(records)
    level_ref[...] = jnp.broadcast_to(records[:, LEVEL : LEVEL + 1], level_ref.shape)
    up_to = [count_ref[octave] for octave in range(4)]
    live_groups = (up_to[3] + GROUP - 1) // GROUP
    pooled_ref[:, FEATURES:] = jnp.zeros((SLOTS, WIDE - FEATURES), BF16)

    def dead_group(group, carry):
        pooled_ref[pl.ds(pl.multiple_of(group * GROUP, GROUP), GROUP), :FEATURES] = jnp.zeros(
            (GROUP, FEATURES), BF16
        )
        return carry

    def one_group(group, carry):
        start = pl.multiple_of(group * GROUP, GROUP)
        rows = pl.ds(start, GROUP)

        @pl.when(start < up_to[0])
        def _():
            coords = coord_ref[rows, :]
            wanted = level_ref[rows, 0:1] == 0.0
            first, count = row_window(coords, wanted)

            @pl.when(count <= 10)
            def _():
                level_block(rows, 0, 512, 512, coords, wanted, jnp.minimum(first, 22))

            @pl.when((count > 10) & (count <= 16))
            def _():
                level_block(rows, 0, 768, 384, coords, wanted, jnp.minimum(first, 16))

            @pl.when(count > 16)
            def _():
                level_block(rows, 0, 1536, 384, coords, wanted)

        @pl.when((start + GROUP > up_to[0]) & (start < up_to[1]))
        def _():
            wanted = level_ref[rows, 0:1] == 1.0
            level_block(
                rows, 1536, 384, 384, coord_ref[rows, :], wanted, begun=start < up_to[0]
            )

        @pl.when((start + GROUP > up_to[1]) & (start < up_to[3]))
        def _():
            wanted = level_ref[rows, :] == table_ref[2:3, 1920:2048]
            level_block(
                rows, 1920, 128, 128, coord_ref[rows, :], wanted, begun=start < up_to[1]
            )

        return carry

    def one_part(part, carry):
        first = part * (SLOT_QUARTER // GROUP)
        last = first + SLOT_QUARTER // GROUP
        live = jnp.maximum(jnp.minimum(last, live_groups), first)
        lax.fori_loop(first, live, one_group, 0)
        lax.fori_loop(live, last, dead_group, 0)
        send(part)
        return carry

    lax.fori_loop(0, SIDE, one_part, 0)


def pooled_copies(pooled_ref, others, sems, way, start, part=None):
    own_x, own_z, own_y = coordinates()
    rows = slice(None) if part is None else pl.ds(part * SLOT_QUARTER, SLOT_QUARTER)
    for axis, (own, width, first) in enumerate(((own_y, PART_Y, 0), (own_z, PART_Z, SPLIT))):
        for chunk in range(SIDE):
            here = pooled_ref.at[rows, first + chunk * width : first + (chunk + 1) * width]

            def copy(place):
                there = others[axis * SIDE + place].at[rows, :]
                ends = (here, there) if way == "out" else (there, here)
                sem = sems.at[axis, chunk] if part is None else sems.at[axis, chunk, part]
                return pltpu.make_async_copy(*ends, sem)

            if not start:
                copy(0).wait()
                continue
            for place in range(SIDE):

                @pl.when((own + place) % SIDE == chunk)
                def _():
                    copy(place).start()


def send_part(pooled_ref, others, sems):
    return lambda part: pooled_copies(pooled_ref, others, sems, "out", True, part)


def wait_parts(pooled_ref, others, sems):
    def one(part, carry):
        pooled_copies(pooled_ref, others, sems, "out", False, part)
        return carry

    lax.fori_loop(0, SIDE, one, 0)


def own_records(record_ref, box_ref):
    lane = lax.broadcasted_iota(jnp.int32, record_ref.shape, 1)
    return jnp.where(lane < 4, box_ref[...], record_ref[...])


def weight_copy(w1_ref, w1_buf, sems, piece):
    rows = pl.ds(pl.multiple_of(piece * PIECE, PIECE), PIECE)
    return pltpu.make_async_copy(w1_ref.at[rows, :], w1_buf.at[rows, :], sems.at[piece])


def first_layer(pooled_ref, w1_ref, w1_buf, sems, b1_ref, pre1, ready):
    pre1[...] = jnp.broadcast_to(b1_ref[...], pre1.shape)

    def one_piece(piece, carry):
        ready(piece)
        weight_copy(w1_ref, w1_buf, sems, piece).wait()
        columns = pl.ds(pl.multiple_of(piece * PIECE, PIECE), PIECE)
        pre1[...] += jnp.dot(pooled_ref[:, columns], w1_buf[columns, :], preferred_element_type=F32)
        return carry

    lax.fori_loop(0, PIECES, one_piece, 0)


def later_layers(
    section, records, pre1, pre2, act1, act2, pred, next_ref, w2_ref, b2_ref, wp_ref, bp_ref, done
):
    done(0)
    act1[...] = gelu(pre1[...]).astype(BF16)
    done(2)
    pre2[...] = jnp.dot(act1[...], w2_ref[...], preferred_element_type=F32) + b2_ref[...]
    done(1)
    act2[...] = gelu(pre2[...]).astype(BF16)
    done(3)
    pred[...] = (
        lax.dot_general(act2[...], wp_ref[...], (((1,), (1,)), ((), ())), preferred_element_type=F32)
        + bp_ref[...]
    )
    done(4)
    lane = lax.broadcasted_iota(jnp.int32, records.shape, 1)
    x1, y1, x2, y2 = [records[:, BOX + k : BOX + k + 1] for k in range(4)]
    deltas = [pred[:, CLASSES + k : CLASSES + k + 1] for k in range(4)]
    near, far = (10.0, 5.0) if section == 0 else (20.0, 10.0)
    width, height = x2 - x1, y2 - y1
    center_x, center_y = x1 + 0.5 * width, y1 + 0.5 * height
    new_x = center_x + deltas[0] / near * width
    new_y = center_y + deltas[1] / near * height
    new_width = width * jnp.exp(deltas[2] / far)
    new_height = height * jnp.exp(deltas[3] / far)
    corners = (
        new_x - 0.5 * new_width,
        new_y - 0.5 * new_height,
        new_x + 0.5 * new_width,
        new_y + 0.5 * new_height,
    )
    result = jnp.zeros_like(records)
    for k in range(4):
        result = jnp.where(lane == BOX + k, corners[k], result)
    next_ref[...] = result


KEPT = [((SLOTS, HIDDEN), F32)] * 2 + [((SLOTS, HIDDEN), BF16)] * 2 + [((SLOTS, 128), F32)]
POOL_SCRATCH = [
    pltpu.VMEM((SLOTS, 128), F32),
    pltpu.VMEM((SLOTS, 128), F32),
    pltpu.VMEM((BINS * GROUP, 1536), BF16),
]
POOLED_SCRATCH = [pltpu.VMEM((SLOTS, WIDE), BF16), pltpu.SemaphoreType.DMA((2, SIDE))]
PARTED_SCRATCH = [pltpu.VMEM((SLOTS, WIDE), BF16), pltpu.SemaphoreType.DMA((2, SIDE, SIDE))]
POOLED = [((SLOTS, PART_Y), BF16)] * SIDE + [((SLOTS, PART_Z), BF16)] * SIDE
HEAD_SCRATCH = [
    pltpu.VMEM((FEATURES, HIDDEN), BF16),
    pltpu.VMEM((SLOTS, HIDDEN), F32),
    pltpu.VMEM((SLOTS, HIDDEN), F32),
    pltpu.VMEM((SLOTS, HIDDEN), BF16),
    pltpu.VMEM((SLOTS, HIDDEN), BF16),
    pltpu.VMEM((SLOTS, 128), F32),
    pltpu.SemaphoreType.DMA((PIECES,)),
    pltpu.SemaphoreType.DMA((5,)),
]


def forward_kernel(
    count_ref,
    record_ref,
    map_ref,
    table_ref,
    b1_ref,
    w2_ref,
    b2_ref,
    wp_ref,
    bp_ref,
    w1_ref,
    *refs,
):
    parts, kept_out, next_ref = refs[: 2 * SIDE], refs[2 * SIDE : 2 * SIDE + 5], refs[2 * SIDE + 5]
    refs = refs[2 * SIDE + 6 :]
    pool_scratch, refs = refs[:3], refs[3:]
    pooled_ref, pooled_sems, w1_buf, pre1, pre2, act1, act2, pred, w_sems, sems = refs

    @pl.when(lax.axis_index("section") == 0)
    def _():
        for piece in range(PIECES):
            weight_copy(w1_ref, w1_buf, w_sems, piece).start()
        records = record_ref[...]
        send = send_part(pooled_ref, parts, pooled_sems)
        pool_all(count_ref, records, map_ref, table_ref, *pool_scratch, pooled_ref, send)
        first_layer(pooled_ref, w1_ref, w1_buf, w_sems, b1_ref, pre1, lambda piece: None)
        copies = [
            pltpu.make_async_copy(here, there, sems.at[place])
            for place, (here, there) in enumerate(zip((pre1, pre2, act1, act2, pred), kept_out))
        ]
        later_layers(
            0,
            records,
            pre1,
            pre2,
            act1,
            act2,
            pred,
            next_ref,
            w2_ref,
            b2_ref,
            wp_ref,
            bp_ref,
            lambda place: copies[place].start(),
        )
        for copy in copies:
            copy.wait()
        wait_parts(pooled_ref, parts, pooled_sems)


def run_forward(counts, records, feature_map, table, weights):
    kept = POOLED + KEPT
    return pl.pallas_call(
        forward_kernel,
        out_shape=tuple(jax.ShapeDtypeStruct(*entry) for entry in kept)
        + (jax.ShapeDtypeStruct((SLOTS, 128), F32),),
        in_specs=[SMEM] + [VMEM] * 8 + [HBM],
        out_specs=(HBM,) * len(kept) + (VMEM,),
        scratch_shapes=POOL_SCRATCH + PARTED_SCRATCH + HEAD_SCRATCH,
        compiler_params=PARAMS,
        cost_estimate=pl.CostEstimate(
            flops=16 * 10**9, bytes_accessed=36 * 10**6, transcendentals=5 * 10**5
        ),
        name="run_forward",
    )(counts, records, feature_map, table, *weights)


def pool_kernel(count_ref, record_ref, box_ref, map_ref, table_ref, *refs):
    parts = refs[2 * SIDE : 4 * SIDE]
    *pool_scratch, pooled_ref, pooled_sems = refs[4 * SIDE :]

    @pl.when(lax.axis_index("section") == 1)
    def _():
        records = own_records(record_ref, box_ref)
        send = send_part(pooled_ref, parts, pooled_sems)
        pool_all(count_ref, records, map_ref, table_ref, *pool_scratch, pooled_ref, send)
        wait_parts(pooled_ref, parts, pooled_sems)


def run_pool(counts, records, boxes, feature_map, table, before):
    return pl.pallas_call(
        pool_kernel,
        out_shape=tuple(jax.ShapeDtypeStruct(*entry) for entry in POOLED),
        in_specs=[SMEM] + [VMEM] * 4 + [HBM] * (2 * SIDE),
        out_specs=(HBM,) * (2 * SIDE),
        scratch_shapes=POOL_SCRATCH + PARTED_SCRATCH,
        input_output_aliases={5 + place: place for place in range(2 * SIDE)},
        compiler_params=PARAMS,
        cost_estimate=pl.CostEstimate(flops=8 * 10**9, bytes_accessed=8 * 10**6, transcendentals=0),
        name="run_pool",
    )(counts, records, boxes, feature_map, table, *before)


def head_kernel(
    record_ref, box_ref, b1_ref, w2_ref, b2_ref, wp_ref, bp_ref, w1_ref, *refs
):
    parts, refs = refs[: 2 * SIDE], refs[2 * SIDE + 5 :]
    kept_out, next_ref, refs = refs[:5], refs[5], refs[6:]
    pooled_ref, pooled_sems, w1_buf, pre1, pre2, act1, act2, pred, w_sems, sems = refs

    @pl.when(lax.axis_index("section") == 1)
    def _():
        weight_copy(w1_ref, w1_buf, w_sems, 0).start()
        pooled_copies(pooled_ref, parts, pooled_sems, "in", True)
        weight_copy(w1_ref, w1_buf, w_sems, 1).start()

        def ready(piece):
            @pl.when(piece == 0)
            def _():
                pooled_copies(pooled_ref, parts, pooled_sems, "in", False)
                weight_copy(w1_ref, w1_buf, w_sems, 2).start()

            @pl.when(piece + 3 < PIECES)
            def _():
                weight_copy(w1_ref, w1_buf, w_sems, piece + 3).start()

        first_layer(pooled_ref, w1_ref, w1_buf, w_sems, b1_ref, pre1, ready)
        copies = [
            pltpu.make_async_copy(here, there, sems.at[place])
            for place, (here, there) in enumerate(zip((pre1, pre2, act1, act2, pred), kept_out))
        ]
        later_layers(
            1,
            own_records(record_ref, box_ref),
            pre1,
            pre2,
            act1,
            act2,
            pred,
            next_ref,
            w2_ref,
            b2_ref,
            wp_ref,
            bp_ref,
            lambda place: copies[place].start(),
        )
        for copy in copies:
            copy.wait()


def run_head(records, boxes, weights, parts, kept):
    return pl.pallas_call(
        head_kernel,
        out_shape=tuple(jax.ShapeDtypeStruct(*entry) for entry in KEPT)
        + (jax.ShapeDtypeStruct((SLOTS, 128), F32),),
        in_specs=[VMEM] * 7 + [HBM] * (1 + 2 * SIDE + 5),
        out_specs=(HBM,) * 5 + (VMEM,),
        scratch_shapes=POOLED_SCRATCH + HEAD_SCRATCH,
        input_output_aliases={8 + 2 * SIDE + place: place for place in range(5)},
        compiler_params=PARAMS,
        cost_estimate=pl.CostEstimate(
            flops=10**10, bytes_accessed=40 * 10**6, transcendentals=6 * 10**5
        ),
        name="run_head",
    )(records, boxes, *weights, *parts, *kept)


def put_parts(values, high_ref, low_ref):
    high = values.astype(BF16)
    high_ref[...] = high
    low_ref[...] = (values - high.astype(F32)).astype(BF16)


def put_tail(target, bias, boxes):
    target[:, 512:] = jnp.zeros((TAIL, target.shape[1] - 512), BF16)
    put_parts(bias, target.at[:, 0:256], target.at[:, 256:512])
    put_parts(boxes, target.at[:, 512:528], target.at[:, 528:544])


def pass_tail(target, bias, back_ref, own):
    target[:, 640:] = jnp.zeros((TAIL, target.shape[1] - 640), BF16)
    put_parts(bias, target.at[:, 0:256], target.at[:, 256:512])
    target[:, 512:640] = back_ref[pl.ds(own, 16, stride=SIDE), :].astype(BF16)


def take_tails(tails, back_ref):
    for k, tail in enumerate(tails):
        back_ref[k * 16 : (k + 1) * 16, :] = tail[:, 512:640].astype(F32)
    near, here, far, across = [
        tail[:, 0:256].astype(F32) + tail[:, 256:512].astype(F32) for tail in tails
    ]
    return (near + far) + (here + across)


def slope_kernel(
    record_ref,
    place_ref,
    next0_ref,
    next1_ref,
    pred,
    pre1,
    pre2,
    act1,
    act2,
    w2_ref,
    wp_ref,
    grad_ref,
    turned_ref,
    c0,
    c1,
    c2,
    c3,
    extra_ref,
    bias_ref,
    back_ref,
    sorted_ref,
):
    own_x, own_z, own_y = coordinates()
    first_section = lax.axis_index("section") == 0
    factor = jnp.where(first_section, 1.0, 0.5).astype(F32)
    records = record_ref[...]
    values = pred[...]
    lane = lax.broadcasted_iota(jnp.int32, values.shape, 1)
    is_class = lane < CLASSES
    peak = jnp.max(jnp.where(is_class, values, -jnp.inf), axis=1, keepdims=True)
    shares = jnp.where(is_class, jnp.exp(values - peak), 0.0)
    shares = shares / jnp.sum(shares, axis=1, keepdims=True)
    label = records[:, LABEL : LABEL + 1]
    weight = factor * records[:, LIVE : LIVE + 1]
    truth = jnp.where(lane.astype(F32) == label, 1.0, 0.0)
    aims = jnp.zeros_like(values)
    for k in range(4):
        aims = jnp.where(lane == CLASSES + k, records[:, TARGET + k : TARGET + k + 1], aims)
    pull = jnp.minimum(jnp.maximum(values - aims, -1.0), 1.0)
    pull = jnp.where(lane < PRED, pull, 0.0) * jnp.where(label > 0.0, 1.0, 0.0)
    out_grad = (jnp.where(is_class, shares - truth, pull) * weight).astype(BF16)
    pred_bias = jnp.sum(out_grad.astype(F32), axis=0, keepdims=True)
    second = jnp.dot(out_grad, wp_ref[...], preferred_element_type=F32)
    second = (second * gelu_slope(pre2[...])).astype(BF16)
    second_bias = jnp.sum(second.astype(F32), axis=0, keepdims=True)
    first = lax.dot_general(
        second, w2_ref[...], (((1,), (1,)), ((), ())), preferred_element_type=F32
    )
    first = (first * gelu_slope(pre1[...])).astype(BF16)
    grad_ref[...] = first
    wide = first.astype(F32)
    first_bias = jnp.sum(wide, axis=0, keepdims=True)
    turned = wide.T.astype(BF16)
    turned_ref[...] = turned
    second_turned = second.astype(F32).T.astype(BF16)
    extra_ref[:, :HIDDEN] = jnp.dot(
        second_turned, act1[...], preferred_element_type=F32
    ).astype(BF16)
    act2_turned = act2[...].astype(F32).T.astype(BF16)
    extra_ref[:, HIDDEN:] = jnp.dot(
        act2_turned, out_grad, preferred_element_type=F32
    ).astype(BF16)
    bias_ref[...] = jnp.zeros_like(bias_ref)
    for row in range(4):
        bias_ref[row : row + 1, :] = first_bias[:, row * 256 : (row + 1) * 256]
        bias_ref[4 + row : 5 + row, :] = second_bias[:, row * 256 : (row + 1) * 256]
    bias_ref[8:9, :128] = pred_bias
    order = jnp.where(
        lax.broadcasted_iota(jnp.int32, (SLOTS, SLOTS), 1).astype(F32) == place_ref[:, 0:1],
        1.0,
        0.0,
    )
    mine = jnp.where(first_section, next0_ref[...], next1_ref[...])
    boxes = jnp.dot(order, mine, precision=EXACT, preferred_element_type=F32)
    small_lane = lax.broadcasted_iota(jnp.int32, (GROUPS, 128), 1)
    back = jnp.zeros((GROUPS, 128), F32)
    for c in range(4):
        for k in range(4):
            back = jnp.where(
                small_lane == 4 * c + k, boxes[c * GROUPS : (c + 1) * GROUPS, k : k + 1], back
            )
    back_ref[...] = back
    for x in range(SIDE):
        for y in range(SIDE):
            sorted_ref[(x * SIDE + y) * SIDE : (x * SIDE + y + 1) * SIDE, :] = back_ref[
                pl.ds(x * 16 + y, SIDE, stride=SIDE), :
            ]
    for jx, target in enumerate((c0, c1, c2, c3)):
        for jz in range(SIDE):
            for jy in range(SIDE):
                source = (
                    (own_x + jx) % SIDE * 256 + (own_z + jz) % SIDE * 64 + (own_y + jy) % SIDE * 16
                )
                to = (jz * SIDE + jy) * 16
                target[to : to + 16, :] = extra_ref[pl.ds(pl.multiple_of(source, 16), 16), :]
        rows = pl.ds(pl.multiple_of((own_x + jx) % SIDE * 16, 16), 16)
        put_tail(target.at[256:, :], bias_ref[...], sorted_ref[rows, :16])


def run_slopes(records, places, after_first, after_second, kept, w2, wp):
    pre1, pre2, act1, act2, pred = kept
    return pl.pallas_call(
        slope_kernel,
        out_shape=(
            jax.ShapeDtypeStruct((SLOTS, HIDDEN), BF16),
            jax.ShapeDtypeStruct((HIDDEN, SLOTS), BF16),
        )
        + (jax.ShapeDtypeStruct((256 + TAIL, EXTRA), BF16),) * SIDE,
        in_specs=[VMEM] * 11,
        out_specs=(VMEM,) * 6,
        scratch_shapes=[
            pltpu.VMEM((HIDDEN, EXTRA), BF16),
            pltpu.VMEM((TAIL, 256), F32),
            pltpu.VMEM((GROUPS, 128), F32),
            pltpu.VMEM((GROUPS, 128), F32),
        ],
        compiler_params=PARAMS,
        cost_estimate=pl.CostEstimate(
            flops=10**6, bytes_accessed=10**5, transcendentals=0
        ),
        name="run_slopes",
    )(records, places, after_first, after_second, pred, pre1, pre2, act1, act2, w2, wp)


def pooled_grad_kernel(grad_ref, w1_ref, out_ref, w1_buf, out_buf, w_sems, out_sems):
    def out_copy(piece):
        columns = pl.ds(pl.multiple_of(piece * PIECE, PIECE), PIECE)
        return pltpu.make_async_copy(out_buf.at[piece], out_ref.at[:, columns], out_sems.at[piece])

    for piece in range(3):
        weight_copy(w1_ref, w1_buf, w_sems, piece).start()

    def one_piece(piece, carry):
        @pl.when(piece + 3 < PIECES)
        def _():
            weight_copy(w1_ref, w1_buf, w_sems, piece + 3).start()

        weight_copy(w1_ref, w1_buf, w_sems, piece).wait()
        rows = pl.ds(pl.multiple_of(piece * PIECE, PIECE), PIECE)
        out_buf[piece] = lax.dot_general(
            grad_ref[...], w1_buf[rows, :], (((1,), (1,)), ((), ())), preferred_element_type=F32
        ).astype(BF16)
        out_copy(piece).start()
        return carry

    lax.fori_loop(0, PIECES, one_piece, 0)

    def finish(piece, carry):
        out_copy(piece).wait()
        return carry

    lax.fori_loop(0, PIECES, finish, 0)


def run_pooled_grad(grad, w1):
    return pl.pallas_call(
        pooled_grad_kernel,
        out_shape=jax.ShapeDtypeStruct((SLOTS, FEATURES), BF16),
        in_specs=[VMEM, HBM],
        out_specs=HBM,
        scratch_shapes=[
            pltpu.VMEM((FEATURES, HIDDEN), BF16),
            pltpu.VMEM((PIECES, SLOTS, PIECE), BF16),
            pltpu.SemaphoreType.DMA((PIECES,)),
            pltpu.SemaphoreType.DMA((PIECES,)),
        ],
        compiler_params=PARAMS,
        cost_estimate=pl.CostEstimate(
            flops=2 * SLOTS * FEATURES * HIDDEN, bytes_accessed=33 * 10**6, transcendentals=0
        ),
        name="run_pooled_grad",
    )(grad, w1)


def scatter_kernel(
    count_ref,
    record_ref,
    box_ref,
    table_ref,
    grad_ref,
    out_ref,
    coord_ref,
    spread_ref,
    turned_ref,
    rows_ref,
    grad_buf,
    slot_ref,
    wide_ref,
    sems,
):
    up_to = [count_ref[octave] for octave in range(4)]
    lane = lax.broadcasted_iota(jnp.int32, (1, 128), 1)
    lane_bin = lane // GROUP

    def grad_copy(quarter):
        rows = pl.ds(pl.multiple_of(quarter * SLOT_QUARTER, SLOT_QUARTER), SLOT_QUARTER)
        return pltpu.make_async_copy(grad_ref.at[rows, :], grad_buf.at[rows, :], sems.at[quarter])

    for quarter in range(SIDE):
        grad_copy(quarter).start()
    out_ref[...] = jnp.zeros_like(out_ref)
    rows_ref[...] = jnp.zeros_like(rows_ref)
    records = record_ref[...]
    wide_lane = lax.broadcasted_iota(jnp.int32, records.shape, 1)
    passed = (wide_lane < 4) & (lax.axis_index("section") == 1)
    records = jnp.where(passed, box_ref[...], records)
    coords = sample_coordinates(records)
    coords = jnp.where(wide_lane == 32, records[:, LEVEL : LEVEL + 1], coords)
    slot_ref[...] = coords
    left = coords.T[:48, :]
    repeat = jnp.where(
        lax.broadcasted_iota(jnp.int32, (SLOTS, 2048), 0)
        == lax.broadcasted_iota(jnp.int32, (SLOTS, 2048), 1) // 128 * GROUP
        + lax.broadcasted_iota(jnp.int32, (SLOTS, 2048), 1) % GROUP,
        1.0,
        0.0,
    ).astype(BF16)
    wide = jnp.zeros((48, 2048), F32)
    for _ in range(3):
        part = left.astype(BF16)
        left = left - part.astype(F32)
        wide = wide + jnp.dot(part, repeat, preferred_element_type=F32)
    wide_ref[...] = wide

    def one_quarter(quarter, carry):
        grad_copy(quarter).wait()
        first = quarter * (SLOT_QUARTER // GROUP)
        live = (up_to[3] + GROUP - 1) // GROUP
        lax.fori_loop(first, jnp.minimum(first + SLOT_QUARTER // GROUP, live), one_group, 0)
        return carry

    def one_group(group, carry):
        start = pl.multiple_of(group * GROUP, GROUP)
        coords = slot_ref[pl.ds(start, GROUP), :]
        coord_ref[...] = wide_ref[:, pl.ds(pl.multiple_of(group * 128, 128), 128)]
        for p in range(7):
            for q in range(7):
                spot = p * 7 + q
                rows_ref[p * 128 + q * GROUP : p * 128 + (q + 1) * GROUP, :] = grad_buf[
                    pl.ds(start, GROUP), spot * CHANNELS : (spot + 1) * CHANNELS
                ]

        def column_ends():
            ends = []
            for side in range(2):
                value = jnp.full((1, 128), -2000.0, F32)
                for q in range(7):
                    row = 16 + 2 * q + side
                    value = jnp.where(lane_bin == q, coord_ref[row : row + 1, :], value)
                ends.append(value)
            return ends

        def ends_of_row(p):
            return coord_ref[2 * p : 2 * p + 1, :], coord_ref[2 * p + 1 : 2 * p + 2, :]

        def grid_block(height, first_row):
            width = 48
            left, right = column_ends()
            wanted = coord_ref[32:33, :] == 0.0
            x_cells = 0.5 * lax.broadcasted_iota(jnp.int32, (width, 128), 0).astype(F32)
            y_cells = 0.5 * (
                lax.broadcasted_iota(jnp.int32, (height, 128), 0) + first_row
            ).astype(F32)
            columns = jnp.where(wanted, tent_pair(left, right, x_cells), 0.0)
            cells = height * width
            for p in range(7):
                top, bottom = ends_of_row(p)
                spread_ref[:height, :] = tent_pair(top, bottom, y_cells)
                for y in range(height):
                    turned_ref[y * width : (y + 1) * width, p * 128 : (p + 1) * 128] = (
                        spread_ref[y : y + 1, :] * columns
                    ).astype(BF16)
            out_ref[pl.ds(pl.multiple_of(first_row * 48, 16), cells), :] += jnp.dot(
                turned_ref[:cells, :], rows_ref[...], preferred_element_type=F32
            )

        @pl.when(start < up_to[0])
        def _():
            first, count = row_window(coords, coords[:, 32:33] == 0.0)

            @pl.when(count <= 10)
            def _():
                grid_block(10, jnp.minimum(first, 22))

            @pl.when((count > 10) & (count <= 20))
            def _():
                grid_block(20, jnp.minimum(first, 12))

            @pl.when(count > 20)
            def _():
                grid_block(32, jnp.int32(0))

        @pl.when((start + GROUP > up_to[0]) & (start < up_to[1]))
        def _():
            left, right = column_ends()
            wanted = coord_ref[32:33, :] == 1.0
            x_cells = 0.5 * lax.broadcasted_iota(jnp.int32, (24, 128), 0).astype(F32)
            y_cells = 0.5 * lax.broadcasted_iota(jnp.int32, (16, 128), 0).astype(F32)
            columns = jnp.where(wanted, tent_pair(left, right, x_cells), 0.0)
            for p in range(7):
                top, bottom = ends_of_row(p)
                spread_ref[:16, :] = tent_pair(top, bottom, y_cells)
                for y in range(0, 16, 2):
                    both = jnp.concatenate(
                        [spread_ref[y : y + 1, :] * columns, spread_ref[y + 1 : y + 2, :] * columns],
                        axis=0,
                    )
                    turned_ref[y * 24 : (y + 2) * 24, p * 128 : (p + 1) * 128] = both.astype(BF16)
            out_ref[1536:1920, :] += jnp.dot(
                turned_ref[:384, :], rows_ref[...], preferred_element_type=F32
            )

        @pl.when((start + GROUP > up_to[1]) & (start < up_to[3]))
        def _():
            left, right = column_ends()
            y_cells = table_ref[:, 0:1]
            x_cells = table_ref[:, 1:2]
            wanted = coord_ref[32:33, :] == table_ref[:, 2:3]
            columns = jnp.where(wanted, tent_pair(left, right, x_cells), 0.0)
            for p in range(7):
                top, bottom = ends_of_row(p)
                turned_ref[:128, p * 128 : (p + 1) * 128] = (
                    tent_pair(top, bottom, y_cells) * columns
                ).astype(BF16)
            update = jnp.dot(turned_ref[:128, :], rows_ref[...], preferred_element_type=F32)
            out_ref[1920:CELLS, :] += update[: CELLS - 1920, :]

        return carry

    lax.fori_loop(0, SIDE, one_quarter, 0)


def run_scatter(counts, records, boxes, table, pooled_grad):
    return pl.pallas_call(
        scatter_kernel,
        out_shape=jax.ShapeDtypeStruct((CELLS, CHANNELS), F32),
        in_specs=[SMEM, VMEM, VMEM, VMEM, HBM],
        out_specs=VMEM,
        scratch_shapes=[
            pltpu.VMEM((48, 128), F32),
            pltpu.VMEM((32, 128), F32),
            pltpu.VMEM((1536, 7 * 128), BF16),
            pltpu.VMEM((7 * 128, CHANNELS), BF16),
            pltpu.VMEM((SLOTS, FEATURES), BF16),
            pltpu.VMEM((SLOTS, 128), F32),
            pltpu.VMEM((48, 2048), F32),
            pltpu.SemaphoreType.DMA((SIDE,)),
        ],
        compiler_params=PARAMS,
        cost_estimate=pl.CostEstimate(
            flops=2 * 10**10, bytes_accessed=9 * 10**6, transcendentals=0
        ),
        name="run_scatter",
    )(counts, records, boxes, table, pooled_grad)


def load_pieces(turned_in, gained, pooled, turned, right, sems, piece_sems, steps):
    sources = [turned_in, *gained]
    first = [
        pltpu.make_async_copy(source, turned.at[k], sems.at[k]) for k, source in enumerate(sources)
    ]
    later = [
        [
            pltpu.make_async_copy(
                pooled[k].at[:, start : start + width],
                right.at[pl.ds(k * SLOTS, SLOTS), start : start + width],
                piece_sems.at[step, k],
            )
            for k in range(SIDE)
        ]
        for step, (start, width) in enumerate(steps)
    ]
    for copy in first:
        copy.start()
    for copies in later:
        for copy in copies:
            copy.start()
    return first, later


def place_left(left, turned, row_of):
    own_x, own_z, own_y = coordinates()
    for j in range(SIDE):
        for i in range(SIDE):
            for h in range(SIDE):
                jx, jz, jy = row_of(j, i, h)
                source = (
                    (own_x + jx) % SIDE * 256 + (own_z + jz) % SIDE * 64 + (own_y + jy) % SIDE * 16
                )
                to = ((j * SIDE + i) * SIDE + h) * 16
                for k in range(SIDE):
                    left[to : to + 16, k * SLOTS : (k + 1) * SLOTS] = turned[
                        k, pl.ds(pl.multiple_of(source, 16), 16), :
                    ]


def multiply(left, right, part, start, width):
    def one(step, carry):
        columns = pl.ds(pl.multiple_of(start + step * 256, 128), 256)
        value = jnp.dot(left[...], right[:, columns], preferred_element_type=F32).astype(BF16)
        for j in range(SIDE):
            part[j, :256, columns] = value[j * 256 : (j + 1) * 256, :]
        return carry

    lax.fori_loop(0, width // 256, one, 0)
    if width % 256:
        end = start + width
        value = jnp.dot(
            left[...], right[:, end - 128 : end], preferred_element_type=F32
        ).astype(BF16)
        for j in range(SIDE):
            part[j, :256, end - 128 : end] = value[j * 256 : (j + 1) * 256, :]


STEPS_Y = ((0, 512), (512, 512))
STEPS_Z = ((0, 1024), (1024, 1152))


def weight_grad_kernel(steps, row_of, extra_count, *refs):
    turned_in, gained, pooled = refs[0], refs[1:4], refs[4:8]
    extras, refs = refs[8 : 8 + extra_count], refs[8 + extra_count :]
    outs, (turned, right, left, part, sems, piece_sems, out_sems) = refs[:SIDE], refs[SIDE:]
    added = [
        pltpu.make_async_copy(extra, part.at[j, :, PART_Y:], out_sems.at[SIDE + j])
        for j, extra in enumerate(extras)
    ]
    for copy in added:
        copy.start()
    first, later = load_pieces(turned_in, gained, pooled, turned, right, sems, piece_sems, steps)
    for copy in first:
        copy.wait()
    place_left(left, turned, row_of)
    for copies, (start, width) in zip(later, steps):
        for copy in copies:
            copy.wait()
        multiply(left, right, part, start, width)
    for copy in added:
        copy.wait()
    results = [pltpu.make_async_copy(part.at[j], outs[j], out_sems.at[j]) for j in range(SIDE)]
    for copy in results:
        copy.start()
    for copy in results:
        copy.wait()


def run_weight_grad(name, steps, row_of, turned, gained, pooled, extra=()):
    width = pooled[0].shape[1]
    shape = (256 + TAIL, width + EXTRA) if extra else (256, width)
    return pl.pallas_call(
        lambda *refs: weight_grad_kernel(steps, row_of, len(extra), *refs),
        out_shape=(jax.ShapeDtypeStruct(shape, BF16),) * SIDE,
        in_specs=[HBM] * (8 + len(extra)),
        out_specs=(HBM,) * SIDE,
        scratch_shapes=[
            pltpu.VMEM((SIDE, HIDDEN, SLOTS), BF16),
            pltpu.VMEM((HIDDEN, width), BF16),
            pltpu.VMEM((HIDDEN, HIDDEN), BF16),
            pltpu.VMEM((SIDE, *shape), BF16),
            pltpu.SemaphoreType.DMA((SIDE,)),
            pltpu.SemaphoreType.DMA((len(steps), SIDE)),
            pltpu.SemaphoreType.DMA((2 * SIDE,)),
        ],
        compiler_params=PARAMS,
        cost_estimate=pl.CostEstimate(
            flops=3 * HIDDEN * HIDDEN * width, bytes_accessed=9 * 10**6, transcendentals=0
        ),
        name=name,
    )(turned, *gained, *pooled, *extra)


def add_rows(ins, rows):
    total = ins[0][rows, :].astype(F32)
    for k in range(1, SIDE):
        total += ins[k][rows, :].astype(F32)
    return total


def sum_y_first_kernel(*refs):
    ins, outs, back_ref = refs[:SIDE], refs[SIDE : 2 * SIDE], refs[2 * SIDE]
    own_x, own_z, own_y = coordinates()
    bias = take_tails([part.at[256:, PART_Y:] for part in ins], back_ref)
    for j in range(SIDE):
        outs[j][:64, :] = add_rows(ins, slice(64 * j, 64 * (j + 1))).astype(BF16)
        outs[j][64:, :PART_Y] = jnp.zeros((TAIL, PART_Y), BF16)
        pass_tail(outs[j].at[64:, PART_Y:], bias, back_ref, (own_z + j) % SIDE)


def sum_y_first(parts):
    return pl.pallas_call(
        sum_y_first_kernel,
        out_shape=(jax.ShapeDtypeStruct((64 + TAIL, WIDE_Y), BF16),) * SIDE,
        in_specs=[VMEM] * SIDE,
        out_specs=(VMEM,) * SIDE,
        scratch_shapes=[pltpu.VMEM((GROUPS, 128), F32)],
        compiler_params=SMALL,
        cost_estimate=pl.CostEstimate(flops=10**6, bytes_accessed=4 * 10**6, transcendentals=0),
        name="sum_y_first",
    )(*parts)


def sum_y_second_kernel(*refs):
    ins, outs, back_ref = refs[:SIDE], refs[SIDE : 2 * SIDE], refs[2 * SIDE]
    own_x, own_z, own_y = coordinates()
    bias = take_tails([part.at[64:, PART_Y:] for part in ins], back_ref)
    for j in range(SIDE):
        outs[j][:16, :] = add_rows(ins, slice(16 * j, 16 * (j + 1))).astype(BF16)
        outs[j][16:, :PART_Y] = jnp.zeros((TAIL, PART_Y), BF16)
        pass_tail(outs[j].at[16:, PART_Y:], bias, back_ref, (own_y + j) % SIDE)


def sum_y_second(parts):
    return pl.pallas_call(
        sum_y_second_kernel,
        out_shape=(jax.ShapeDtypeStruct((16 + TAIL, WIDE_Y), BF16),) * SIDE,
        in_specs=[VMEM] * SIDE,
        out_specs=(VMEM,) * SIDE,
        scratch_shapes=[pltpu.VMEM((GROUPS, 128), F32)],
        compiler_params=SMALL,
        cost_estimate=pl.CostEstimate(flops=10**6, bytes_accessed=10**6, transcendentals=0),
        name="sum_y_second",
    )(*parts)


def sum_z_kernel(rows, *refs):
    ins, outs = refs[:SIDE], refs[SIDE:]
    for j in range(SIDE):
        outs[j][...] = add_rows(ins, slice(rows * j, rows * (j + 1))).astype(BF16)


def sum_z(parts):
    rows = parts[0].shape[0] // SIDE
    return pl.pallas_call(
        lambda *refs: sum_z_kernel(rows, *refs),
        out_shape=(jax.ShapeDtypeStruct((rows, PART_Z), BF16),) * SIDE,
        in_specs=[VMEM] * SIDE,
        out_specs=(VMEM,) * SIDE,
        compiler_params=SMALL,
        cost_estimate=pl.CostEstimate(flops=10**6, bytes_accessed=10**6, transcendentals=0),
        name="sum_z",
    )(*parts)


def join_kernel(image_ref, *refs):
    parts_y, parts_z = refs[:SIDE], refs[SIDE : 2 * SIDE]
    out_ref, second_ref, pred_ref, first_bias, second_bias, pred_bias, refined_ref = refs[
        2 * SIDE : 2 * SIDE + 7
    ]
    back_ref, bias_ref = refs[2 * SIDE + 7 :]
    own_x, own_z, own_y = coordinates()
    for parts, own, width, first in (
        (parts_y, own_y, PART_Y, 0),
        (parts_z, own_z, PART_Z, SPLIT),
    ):
        for k in range(SIDE):
            for chunk in range(SIDE):
                start = first + chunk * width
                count = min(width, FEATURES - start)

                @pl.when((own - k + SIDE) % SIDE == chunk)
                def _():
                    out_ref[:, start : start + count] = parts[k][:16, :count].astype(F32)

    extra = [part.at[:, PART_Y:] for part in parts_y]
    total = add_rows(extra, slice(0, 16))
    second_ref[...] = total[:, :HIDDEN]
    pred_ref[...] = total[:, HIDDEN:]
    bias_ref[...] = take_tails([part.at[16:, :] for part in extra], back_ref)
    for row in range(4):
        lanes = slice(row * 256, (row + 1) * 256)
        first_bias[:, lanes] = bias_ref[row : row + 1, :]
        second_bias[:, lanes] = bias_ref[4 + row : 5 + row, :]
    pred_bias[...] = bias_ref[8:9, :128]
    images = image_ref[...]
    slot = slot_of_regions(images.astype(F32))
    owner = (
        jnp.bitwise_and(own_y - images, 3) * 16
        + jnp.bitwise_and(own_z - (images >> 2), 3) * 4
        + jnp.bitwise_and(own_x - (images >> 4), 3)
    )
    chosen = jnp.where(lax.broadcasted_iota(jnp.int32, (GROUPS, REGIONS), 0) == owner, 1.0, 0.0)
    values = jnp.dot(back_ref[...].T, chosen, precision=EXACT, preferred_element_type=F32)
    values = values[:16, :] + values[16:32, :]
    result = jnp.zeros((4, REGIONS), F32)
    for c in range(4):
        result = jnp.where(slot == float(c), values[4 * c : 4 * c + 4, :], result)
    refined_ref[...] = result


def join_parts(images, parts_y, parts_z):
    return pl.pallas_call(
        join_kernel,
        out_shape=(
            jax.ShapeDtypeStruct((16, FEATURES), F32),
            jax.ShapeDtypeStruct((16, HIDDEN), F32),
            jax.ShapeDtypeStruct((16, 128), F32),
            jax.ShapeDtypeStruct((1, HIDDEN), F32),
            jax.ShapeDtypeStruct((1, HIDDEN), F32),
            jax.ShapeDtypeStruct((1, 128), F32),
            jax.ShapeDtypeStruct((4, REGIONS), F32),
        ),
        in_specs=[VMEM] * (1 + 2 * SIDE),
        out_specs=(VMEM,) * 7,
        scratch_shapes=[pltpu.VMEM((GROUPS, 128), F32), pltpu.VMEM((TAIL, 256), F32)],
        compiler_params=SMALL,
        cost_estimate=pl.CostEstimate(flops=10**6, bytes_accessed=2 * 10**6, transcendentals=0),
        name="join_parts",
    )(images, *parts_y, *parts_z)


def ring(arrays, axis):
    return [arrays[0]] + [shift(arrays[by], axis, by) for by in range(1, SIDE)]


def body(
    pyramid,
    boxes,
    image_ids,
    levels,
    labels,
    targets,
    w_first,
    b_first,
    w_second,
    b_second,
    w_pred,
    b_pred,
):
    rows, cols, cell_levels = cell_tables()
    lane_table = jnp.asarray(np.stack([rows, cols, cell_levels] + [np.zeros_like(rows)] * 5))
    side_table = np.zeros((128, 128), np.float32)
    side_table[:, 0], side_table[:, 1], side_table[:, 2] = (
        rows[1920:],
        cols[1920:],
        cell_levels[1920:],
    )
    side_table = jnp.asarray(side_table)
    feature_map = jnp.pad(pyramid[0], ((0, CELLS_PAD - CELLS), (0, 0)))
    pred_weight = jnp.pad(w_pred[0], ((0, 128 - PRED), (0, 0)))
    pred_bias = jnp.pad(b_pred, ((0, 0), (0, 128 - PRED)))
    image_row = image_ids.reshape(1, REGIONS)

    with jax.named_scope("regions_to_images"):
        sent = send_regions(image_row, boxes, levels.reshape(1, REGIONS), labels, targets[0])
        got = lax.all_to_all(sent, "region", 0, 0, tiled=True)
    records, places, counts = select_slots(got)
    weights = (b_first, w_second[0], b_second, pred_weight, pred_bias, w_first[0])

    *kept, after_first = run_forward(counts, records, feature_map, lane_table, weights)
    with jax.named_scope("boxes_to_second"):
        passed = lax.ppermute(after_first, "section", [(0, 1)])
    kept, pooled = kept[2 * SIDE :], kept[: 2 * SIDE]
    pooled = run_pool(counts, records, passed, feature_map, lane_table, pooled)
    with jax.named_scope("pooled_over_rings"):
        pooled_y = ring(pooled[:SIDE], "y")
        pooled_z = [pooled[SIDE]] + [shift(pooled[SIDE + by], "z", by) for by in (1, 3)]
    *kept, after_second = run_head(records, passed, weights, pooled, kept)
    grad, turned, *extra = run_slopes(
        records, places, after_first, after_second, kept, w_second[0], pred_weight
    )
    *joined, last, grad = lax.optimization_barrier(
        (*pooled_y, *pooled_z, pooled[SIDE + 2], grad)
    )
    pooled_y, pooled_z = joined[:SIDE], joined[SIDE:]
    with jax.named_scope("pooled_over_rings"):
        pooled_z.insert(2, shift(last, "z", 2))
    with jax.named_scope("gradient_over_rings"):
        gained_y = ring([turned] * SIDE, "y")[1:]
        gained_z = [shift(turned, "z", 1)]
    pooled_grad = run_pooled_grad(grad, w_first[0])
    *gained_z, pooled_z[2], pooled_grad, turned = lax.optimization_barrier(
        (*gained_z, pooled_z[2], pooled_grad, turned)
    )
    with jax.named_scope("gradient_over_rings"):
        gained_z += [shift(turned, "z", by) for by in (2, 3)]
    part_y = run_weight_grad(
        "run_grad_y", STEPS_Y, lambda j, i, h: (j, i, h), turned, gained_y, pooled_y, extra
    )
    *part_y, turned = lax.optimization_barrier((*part_y, turned))
    part_z = run_weight_grad(
        "run_grad_z", STEPS_Z, lambda j, i, h: (i, h, j), turned, gained_z, pooled_z
    )
    *part_z, pooled_grad = lax.optimization_barrier((*part_z, pooled_grad))
    map_grad = run_scatter(counts, records, passed, side_table, pooled_grad)
    with jax.named_scope("sum_over_rings"):
        part_y, part_z = ring(part_y, "x"), ring(part_z, "y")
        part_y[0], part_z[0], map_grad = lax.optimization_barrier((part_y[0], part_z[0], map_grad))
        part_y = ring(sum_y_first(part_y), "z")
        part_z = ring(sum_z(part_z), "x")
        part_y, part_z = sum_y_second(part_y), sum_z(part_z)
    with jax.named_scope("columns_over_rings"):
        first, second, pred, first_bias, second_bias, bias, refined = join_parts(
            image_row, ring(part_y, "y"), ring(part_z, "z")
        )
    return (
        first.T[None],
        first_bias,
        second.T[None],
        second_bias,
        pred[:, :PRED].T[None],
        bias[:, :PRED],
        map_grad[None, None],
        refined[None],
    )


def solution(mesh):
    return jax.shard_map(
        body,
        mesh=mesh,
        in_specs=(
            P("region", None, None),
            P(None, "region"),
            P("region", None),
            P("region"),
            P("section", "region"),
            P("section", None, "region"),
            P("section", None, None),
            P("section", None),
            P("section", None, None),
            P("section", None),
            P("section", None, None),
            P("section", None),
        ),
        out_specs=(
            P("section", None, "region"),
            P("section", None),
            P("section", None, "region"),
            P("section", None),
            P("section", None, "region"),
            P("section", None),
            P("section", "region", None, None),
            P("section", None, "region"),
        ),
        check_vma=False,
    )
```

```python
import jax
import jax.numpy as jnp
import numpy as np
from jax import lax
from jax.experimental import pallas as pl
from jax.experimental.pallas import tpu as pltpu
from jax.sharding import PartitionSpec as P

SIDE = 4
GROUPS = 64
SLOTS = 256
GROUP = 16
SLOT_QUARTER = 64
REGIONS = 128
CHANNELS = 256
BINS = 49
FEATURES = 12544
HIDDEN = 1024
CLASSES = 81
PRED = 85
PART_Y = 1024
PART_Z = 2176
SPLIT = SIDE * PART_Y
WIDE = SPLIT + SIDE * PART_Z
EXTRA = HIDDEN + 128
TAIL = 16
WIDE_Y = PART_Y + EXTRA
CELLS = 2040
CELLS_PAD = 2048
EXACT = lax.Precision.HIGHEST
F32 = jnp.float32
BF16 = jnp.bfloat16
HBM = pl.BlockSpec(memory_space=pltpu.HBM)
VMEM = pl.BlockSpec(memory_space=pltpu.VMEM)
SMEM = pl.BlockSpec(memory_space=pltpu.SMEM)
MIB = 1 << 20
PARAMS = pltpu.CompilerParams(vmem_limit_bytes=60 * MIB)
SMALL = pltpu.CompilerParams(vmem_limit_bytes=16 * MIB)

BOX, LEVEL, LABEL, TARGET, LIVE = 0, 4, 5, 6, 10
FIELDS = 16


def ring_pairs(axis, by):
    step = {"x": 16, "z": 4, "y": 1}[axis]
    pairs = []
    for source in range(GROUPS):
        place = source // step % SIDE
        pairs.append((source, source + ((place + by) % SIDE - place) * step))
    return pairs


def shift(array, axis, by):
    return lax.ppermute(array, "region", ring_pairs(axis, by))


def coordinates():
    own = lax.axis_index("region")
    return own // 16, own // 4 % SIDE, own % SIDE


def cell_tables():
    rows = np.full((CELLS_PAD,), -1000.0, np.float32)
    cols = np.full((CELLS_PAD,), -1000.0, np.float32)
    levels = np.full((CELLS_PAD,), -1.0, np.float32)
    start = 0
    for octave in range(4):
        height, width = 32 >> octave, 48 >> octave
        spots = np.arange(height * width)
        rows[start : start + height * width] = 0.5 * (spots // width)
        cols[start : start + height * width] = 0.5 * (spots % width)
        levels[start : start + height * width] = octave
        start += height * width
    return rows, cols, levels


def tent_pair(first, second, cells):
    return jnp.maximum(0.5 - jnp.abs(first - cells), 0.0) + jnp.maximum(
        0.5 - jnp.abs(second - cells), 0.0
    )


def sample_coordinates(records):
    lane = lax.broadcasted_iota(jnp.int32, records.shape, 1)
    level = records[:, LEVEL : LEVEL + 1]

    def of_level(values):
        return jnp.where(
            level == 0.0,
            values[0],
            jnp.where(level == 1.0, values[1], jnp.where(level == 2.0, values[2], values[3])),
        ).astype(F32)

    scale = of_level((0.25, 0.125, 0.0625, 0.03125))
    anchors, bins = [], []
    for low in (1, 0):
        lower, upper = records[:, low : low + 1], records[:, low + 2 : low + 3]
        anchors.append(lower * scale - 0.5)
        bins.append((upper - lower) * scale / 7.0)
    along_y = lane < 16
    offset = (jnp.where(along_y, lane, lane - 16).astype(F32) + 0.5) * 0.5
    coords = jnp.where(along_y, anchors[0], anchors[1]) + jnp.where(along_y, bins[0], bins[1]) * offset
    limit = jnp.where(along_y, of_level((31.0, 15.0, 7.0, 3.0)), of_level((47.0, 23.0, 11.0, 5.0)))
    return 0.5 * jnp.minimum(jnp.maximum(coords, 0.0), limit)


def row_window(coords, wanted):
    lane = lax.broadcasted_iota(jnp.int32, coords.shape, 1)
    mine = wanted & (lane < 14)
    low = jnp.min(jnp.where(mine, coords, 1000.0))
    high = jnp.max(jnp.where(mine, coords, -1000.0))
    first = (2.0 * low).astype(jnp.int32)
    return first, (2.0 * high).astype(jnp.int32) + 2 - first


def slot_of_regions(images):
    lane = lax.broadcasted_iota(jnp.int32, (1, REGIONS), 1)
    wide = jnp.broadcast_to(images, (REGIONS, REGIONS))
    row = lax.broadcasted_iota(jnp.int32, (REGIONS, REGIONS), 0)
    column = lax.broadcasted_iota(jnp.int32, (REGIONS, REGIONS), 1)
    earlier = (wide.T == wide) & (row < column) & ((row >= 64) == (column >= 64))
    second = jnp.max(jnp.where(earlier, 1.0, 0.0), axis=0, keepdims=True)
    return jnp.where(lane >= 64, 2.0, 0.0) + second


def send_kernel(image_ref, box_ref, level_ref, label_ref, target_ref, out_ref):
    images = image_ref[...].astype(F32)
    slots = slot_of_regions(images)
    fields = jnp.concatenate(
        [
            box_ref[...],
            level_ref[...].astype(F32),
            label_ref[...].astype(F32),
            target_ref[...],
            jnp.ones((1, REGIONS), F32),
            jnp.zeros((5, REGIONS), F32),
        ],
        axis=0,
    )
    owner = lax.broadcasted_iota(jnp.int32, (GROUPS, REGIONS), 0).astype(F32) == images
    out_ref[...] = jnp.zeros_like(out_ref)
    for c in range(4):
        chosen = jnp.where(owner & (slots == float(c)), 1.0, 0.0)
        out_ref[:, c * FIELDS : (c + 1) * FIELDS] = lax.dot_general(
            chosen, fields, (((1,), (1,)), ((), ())), precision=EXACT, preferred_element_type=F32
        )


def send_regions(images, boxes, levels, labels, targets):
    return pl.pallas_call(
        send_kernel,
        out_shape=jax.ShapeDtypeStruct((GROUPS, 128), F32),
        in_specs=[VMEM] * 5,
        out_specs=VMEM,
        compiler_params=PARAMS,
        cost_estimate=pl.CostEstimate(flops=10**7, bytes_accessed=10**5, transcendentals=0),
        name="send_regions",
    )(images, boxes, levels, labels, targets)


def select_kernel(got_ref, record_ref, place_ref, count_ref, raw_ref):
    raw_ref[...] = jnp.zeros_like(raw_ref)
    for c in range(4):
        raw_ref[c * GROUPS : (c + 1) * GROUPS, :FIELDS] = got_ref[
            :, c * FIELDS : (c + 1) * FIELDS
        ]
    raw = raw_ref[...]
    lane = lax.broadcasted_iota(jnp.int32, (SLOTS, 128), 1)
    raw = jnp.where((lane == LEVEL) & (raw[:, LIVE : LIVE + 1] == 0.0), 4.0, raw)
    turned = raw.T
    spot_col = lax.broadcasted_iota(jnp.int32, (SLOTS, 1), 0).astype(F32)
    spot_row = lax.broadcasted_iota(jnp.int32, (1, SLOTS), 1).astype(F32)
    levels_row = turned[LEVEL : LEVEL + 1, :]
    key_col = raw[:, LEVEL : LEVEL + 1] * 1024.0 + raw[:, 1:2] + raw[:, 3:4]
    key_row = levels_row * 1024.0 + turned[1:2, :] + turned[3:4, :]
    same = key_col == key_row
    col_first = (key_col < key_row) | (same & (spot_col < spot_row))
    row_first = (key_row < key_col) | (same & (spot_row < spot_col))
    place_row = jnp.sum(jnp.where(col_first, 1.0, 0.0), axis=0, keepdims=True)
    place_col = jnp.sum(jnp.where(row_first, 1.0, 0.0), axis=1, keepdims=True)
    order = jnp.where(
        lax.broadcasted_iota(jnp.int32, (SLOTS, SLOTS), 0).astype(F32) == place_row, 1.0, 0.0
    )
    record_ref[...] = jnp.dot(order, raw, precision=EXACT, preferred_element_type=F32)
    place_ref[...] = jnp.broadcast_to(place_col, (SLOTS, 128))
    for octave in range(4):
        count_ref[octave] = jnp.sum(jnp.where(levels_row <= float(octave), 1, 0))


def select_slots(got):
    return pl.pallas_call(
        select_kernel,
        out_shape=(
            jax.ShapeDtypeStruct((SLOTS, 128), F32),
            jax.ShapeDtypeStruct((SLOTS, 128), F32),
            jax.ShapeDtypeStruct((8,), jnp.int32),
        ),
        in_specs=[VMEM],
        out_specs=(VMEM, VMEM, SMEM),
        scratch_shapes=[pltpu.VMEM((SLOTS, 128), F32)],
        compiler_params=SMALL,
        cost_estimate=pl.CostEstimate(flops=10**8, bytes_accessed=10**6, transcendentals=0),
        name="select_slots",
    )(got)


def gelu(values):
    inner = 0.7978845608028654 * (values + 0.044715 * (values * values * values))
    return 0.5 * values * (1.0 + jnp.tanh(inner))


def gelu_slope(values):
    square = values * values
    inner = 0.7978845608028654 * values * (1.0 + 0.044715 * square)
    bend = jnp.tanh(inner)
    slope = 0.7978845608028654 * (1.0 + 3.0 * 0.044715 * square)
    return 0.5 * (1.0 + bend) + 0.5 * values * (1.0 - bend * bend) * slope


PIECE = 1792
PIECES = FEATURES // PIECE


def pool_all(
    count_ref, records, map_ref, table_ref, coord_ref, level_ref, weight_ref, pooled_ref, send
):
    def level_block(rows, first_cell, cells, period, coords, wanted, first_row=None, begun=None):
        map_rows = slice(first_cell, first_cell + cells)
        if first_row is not None:
            map_rows = pl.ds(pl.multiple_of(first_row * 48, 16), cells)
            lane = lax.broadcasted_iota(jnp.int32, coords.shape, 1)
            coords = jnp.where(lane < 16, coords - 0.5 * first_row.astype(F32), coords)
        row_cells = table_ref[0:1, first_cell : first_cell + cells]
        col_cells = table_ref[1:2, first_cell : first_cell + period]
        columns = []
        for q in range(7):
            share = tent_pair(
                coords[:, 16 + 2 * q : 17 + 2 * q], coords[:, 17 + 2 * q : 18 + 2 * q], col_cells
            )
            columns.append(jnp.where(wanted, share, 0.0).astype(BF16))
        for p in range(7):
            share = tent_pair(
                coords[:, 2 * p : 2 * p + 1], coords[:, 2 * p + 1 : 2 * p + 2], row_cells
            ).astype(BF16)
            for q in range(7):
                for part in range(cells // period):
                    weight_ref[
                        (p * 7 + q) * GROUP : (p * 7 + q + 1) * GROUP,
                        part * period : (part + 1) * period,
                    ] = share[:, part * period : (part + 1) * period] * columns[q]
        total = jnp.dot(
            weight_ref[:, :cells], map_ref[map_rows, :], preferred_element_type=F32
        )
        for spot in range(BINS):
            value = total[spot * GROUP : (spot + 1) * GROUP, :]
            place = (rows, slice(spot * CHANNELS, (spot + 1) * CHANNELS))
            if begun is not None:
                value = value + jnp.where(begun, pooled_ref[place].astype(F32), 0.0)
            pooled_ref[place] = value.astype(BF16)

    coord_ref[...] = sample_coordinates(records)
    level_ref[...] = jnp.broadcast_to(records[:, LEVEL : LEVEL + 1], level_ref.shape)
    up_to = [count_ref[octave] for octave in range(4)]
    live_groups = (up_to[3] + GROUP - 1) // GROUP
    pooled_ref[:, FEATURES:] = jnp.zeros((SLOTS, WIDE - FEATURES), BF16)

    def dead_group(group, carry):
        pooled_ref[pl.ds(pl.multiple_of(group * GROUP, GROUP), GROUP), :FEATURES] = jnp.zeros(
            (GROUP, FEATURES), BF16
        )
        return carry

    def one_group(group, carry):
        start = pl.multiple_of(group * GROUP, GROUP)
        rows = pl.ds(start, GROUP)

        @pl.when(start < up_to[0])
        def _():
            coords = coord_ref[rows, :]
            wanted = level_ref[rows, 0:1] == 0.0
            first, count = row_window(coords, wanted)

            @pl.when(count <= 10)
            def _():
                level_block(rows, 0, 512, 512, coords, wanted, jnp.minimum(first, 22))

            @pl.when((count > 10) & (count <= 16))
            def _():
                level_block(rows, 0, 768, 384, coords, wanted, jnp.minimum(first, 16))

            @pl.when(count > 16)
            def _():
                level_block(rows, 0, 1536, 384, coords, wanted)

        @pl.when((start + GROUP > up_to[0]) & (start < up_to[1]))
        def _():
            wanted = level_ref[rows, 0:1] == 1.0
            level_block(
                rows, 1536, 384, 384, coord_ref[rows, :], wanted, begun=start < up_to[0]
            )

        @pl.when((start + GROUP > up_to[1]) & (start < up_to[3]))
        def _():
            wanted = level_ref[rows, :] == table_ref[2:3, 1920:2048]
            level_block(
                rows, 1920, 128, 128, coord_ref[rows, :], wanted, begun=start < up_to[1]
            )

        return carry

    def one_part(part, carry):
        first = part * (SLOT_QUARTER // GROUP)
        last = first + SLOT_QUARTER // GROUP
        live = jnp.maximum(jnp.minimum(last, live_groups), first)
        lax.fori_loop(first, live, one_group, 0)
        lax.fori_loop(live, last, dead_group, 0)
        send(part)
        return carry

    lax.fori_loop(0, SIDE, one_part, 0)


def pooled_copies(pooled_ref, others, sems, way, start, part=None):
    own_x, own_z, own_y = coordinates()
    rows = slice(None) if part is None else pl.ds(part * SLOT_QUARTER, SLOT_QUARTER)
    for axis, (own, width, first) in enumerate(((own_y, PART_Y, 0), (own_z, PART_Z, SPLIT))):
        for chunk in range(SIDE):
            here = pooled_ref.at[rows, first + chunk * width : first + (chunk + 1) * width]

            def copy(place):
                there = others[axis * SIDE + place].at[rows, :]
                ends = (here, there) if way == "out" else (there, here)
                sem = sems.at[axis, chunk] if part is None else sems.at[axis, chunk, part]
                return pltpu.make_async_copy(*ends, sem)

            if not start:
                copy(0).wait()
                continue
            for place in range(SIDE):

                @pl.when((own + place) % SIDE == chunk)
                def _():
                    copy(place).start()


def send_part(pooled_ref, others, sems):
    return lambda part: pooled_copies(pooled_ref, others, sems, "out", True, part)


def wait_parts(pooled_ref, others, sems):
    def one(part, carry):
        pooled_copies(pooled_ref, others, sems, "out", False, part)
        return carry

    lax.fori_loop(0, SIDE, one, 0)


def own_records(record_ref, box_ref):
    lane = lax.broadcasted_iota(jnp.int32, record_ref.shape, 1)
    return jnp.where(lane < 4, box_ref[...], record_ref[...])


def weight_copy(w1_ref, w1_buf, sems, piece):
    rows = pl.ds(pl.multiple_of(piece * PIECE, PIECE), PIECE)
    return pltpu.make_async_copy(w1_ref.at[rows, :], w1_buf.at[rows, :], sems.at[piece])


def later_copies(w2_ref, wp_ref, w2_buf, wp_buf, sems):
    return [
        pltpu.make_async_copy(w2_ref, w2_buf, sems.at[0]),
        pltpu.make_async_copy(wp_ref, wp_buf, sems.at[1]),
    ]


def first_layer(pooled_ref, w1_ref, w1_buf, sems, b1_ref, pre1, ready):
    pre1[...] = jnp.broadcast_to(b1_ref[...], pre1.shape)

    def one_piece(piece, carry):
        ready(piece)
        weight_copy(w1_ref, w1_buf, sems, piece).wait()
        columns = pl.ds(pl.multiple_of(piece * PIECE, PIECE), PIECE)
        pre1[...] += jnp.dot(pooled_ref[:, columns], w1_buf[columns, :], preferred_element_type=F32)
        return carry

    lax.fori_loop(0, PIECES, one_piece, 0)


def later_layers(
    section, records, pre1, pre2, act1, act2, pred, next_ref, w2_ref, b2_ref, wp_ref, bp_ref, done
):
    done(0)
    act1[...] = gelu(pre1[...]).astype(BF16)
    done(2)
    pre2[...] = jnp.dot(act1[...], w2_ref[...], preferred_element_type=F32) + b2_ref[...]
    done(1)
    act2[...] = gelu(pre2[...]).astype(BF16)
    done(3)
    pred[...] = (
        lax.dot_general(act2[...], wp_ref[...], (((1,), (1,)), ((), ())), preferred_element_type=F32)
        + bp_ref[...]
    )
    done(4)
    lane = lax.broadcasted_iota(jnp.int32, records.shape, 1)
    x1, y1, x2, y2 = [records[:, BOX + k : BOX + k + 1] for k in range(4)]
    deltas = [pred[:, CLASSES + k : CLASSES + k + 1] for k in range(4)]
    near, far = (10.0, 5.0) if section == 0 else (20.0, 10.0)
    width, height = x2 - x1, y2 - y1
    center_x, center_y = x1 + 0.5 * width, y1 + 0.5 * height
    new_x = center_x + deltas[0] / near * width
    new_y = center_y + deltas[1] / near * height
    new_width = width * jnp.exp(deltas[2] / far)
    new_height = height * jnp.exp(deltas[3] / far)
    corners = (
        new_x - 0.5 * new_width,
        new_y - 0.5 * new_height,
        new_x + 0.5 * new_width,
        new_y + 0.5 * new_height,
    )
    result = jnp.zeros_like(records)
    for k in range(4):
        result = jnp.where(lane == BOX + k, corners[k], result)
    next_ref[...] = result


KEPT = [((SLOTS, HIDDEN), F32)] * 2 + [((SLOTS, HIDDEN), BF16)] * 2 + [((SLOTS, 128), F32)]
POOL_SCRATCH = [
    pltpu.VMEM((SLOTS, 128), F32),
    pltpu.VMEM((SLOTS, 128), F32),
    pltpu.VMEM((BINS * GROUP, 1536), BF16),
]
POOLED_SCRATCH = [pltpu.VMEM((SLOTS, WIDE), BF16), pltpu.SemaphoreType.DMA((2, SIDE))]
PARTED_SCRATCH = [pltpu.VMEM((SLOTS, WIDE), BF16), pltpu.SemaphoreType.DMA((2, SIDE, SIDE))]
POOLED = [((SLOTS, PART_Y), BF16)] * SIDE + [((SLOTS, PART_Z), BF16)] * SIDE
HEAD_SCRATCH = [
    pltpu.VMEM((FEATURES, HIDDEN), BF16),
    pltpu.VMEM((SLOTS, HIDDEN), F32),
    pltpu.VMEM((SLOTS, HIDDEN), F32),
    pltpu.VMEM((SLOTS, HIDDEN), BF16),
    pltpu.VMEM((SLOTS, HIDDEN), BF16),
    pltpu.VMEM((SLOTS, 128), F32),
    pltpu.SemaphoreType.DMA((PIECES,)),
    pltpu.SemaphoreType.DMA((5,)),
    pltpu.VMEM((HIDDEN, HIDDEN), BF16),
    pltpu.VMEM((128, HIDDEN), BF16),
    pltpu.SemaphoreType.DMA((2,)),
]


def forward_kernel(
    count_ref,
    record_ref,
    map_ref,
    table_ref,
    b1_ref,
    w2_ref,
    b2_ref,
    wp_ref,
    bp_ref,
    w1_ref,
    *refs,
):
    parts, kept_out, next_ref = refs[: 2 * SIDE], refs[2 * SIDE : 2 * SIDE + 5], refs[2 * SIDE + 5]
    refs = refs[2 * SIDE + 6 :]
    pool_scratch, refs = refs[:3], refs[3:]
    pooled_ref, pooled_sems, w1_buf, pre1, pre2, act1, act2, pred, w_sems, sems = refs[:-3]
    later = later_copies(w2_ref, wp_ref, *refs[-3:])

    @pl.when(lax.axis_index("section") == 0)
    def _():
        for piece in range(PIECES):
            weight_copy(w1_ref, w1_buf, w_sems, piece).start()
        for copy in later:
            copy.start()
        records = record_ref[...]
        send = send_part(pooled_ref, parts, pooled_sems)
        pool_all(count_ref, records, map_ref, table_ref, *pool_scratch, pooled_ref, send)
        first_layer(pooled_ref, w1_ref, w1_buf, w_sems, b1_ref, pre1, lambda piece: None)
        for copy in later:
            copy.wait()
        copies = [
            pltpu.make_async_copy(here, there, sems.at[place])
            for place, (here, there) in enumerate(zip((pre1, pre2, act1, act2, pred), kept_out))
        ]
        later_layers(
            0,
            records,
            pre1,
            pre2,
            act1,
            act2,
            pred,
            next_ref,
            refs[-3],
            b2_ref,
            refs[-2],
            bp_ref,
            lambda place: copies[place].start(),
        )
        for copy in copies:
            copy.wait()
        wait_parts(pooled_ref, parts, pooled_sems)


def run_forward(counts, records, feature_map, table, weights):
    kept = POOLED + KEPT
    return pl.pallas_call(
        forward_kernel,
        out_shape=tuple(jax.ShapeDtypeStruct(*entry) for entry in kept)
        + (jax.ShapeDtypeStruct((SLOTS, 128), F32),),
        in_specs=[SMEM] + [VMEM] * 4 + [HBM, VMEM, HBM, VMEM, HBM],
        out_specs=(HBM,) * len(kept) + (VMEM,),
        scratch_shapes=POOL_SCRATCH + PARTED_SCRATCH + HEAD_SCRATCH,
        compiler_params=PARAMS,
        cost_estimate=pl.CostEstimate(
            flops=16 * 10**9, bytes_accessed=36 * 10**6, transcendentals=5 * 10**5
        ),
        name="run_forward",
    )(counts, records, feature_map, table, *weights)


def pool_kernel(count_ref, record_ref, box_ref, map_ref, table_ref, *refs):
    parts = refs[2 * SIDE : 4 * SIDE]
    *pool_scratch, pooled_ref, pooled_sems = refs[4 * SIDE :]

    @pl.when(lax.axis_index("section") == 1)
    def _():
        records = own_records(record_ref, box_ref)
        send = send_part(pooled_ref, parts, pooled_sems)
        pool_all(count_ref, records, map_ref, table_ref, *pool_scratch, pooled_ref, send)
        wait_parts(pooled_ref, parts, pooled_sems)


def run_pool(counts, records, boxes, feature_map, table, before):
    return pl.pallas_call(
        pool_kernel,
        out_shape=tuple(jax.ShapeDtypeStruct(*entry) for entry in POOLED),
        in_specs=[SMEM] + [VMEM] * 4 + [HBM] * (2 * SIDE),
        out_specs=(HBM,) * (2 * SIDE),
        scratch_shapes=POOL_SCRATCH + PARTED_SCRATCH,
        input_output_aliases={5 + place: place for place in range(2 * SIDE)},
        compiler_params=PARAMS,
        cost_estimate=pl.CostEstimate(flops=8 * 10**9, bytes_accessed=8 * 10**6, transcendentals=0),
        name="run_pool",
    )(counts, records, boxes, feature_map, table, *before)


def head_kernel(
    record_ref, box_ref, b1_ref, w2_ref, b2_ref, wp_ref, bp_ref, w1_ref, *refs
):
    parts, refs = refs[: 2 * SIDE], refs[2 * SIDE + 5 :]
    kept_out, next_ref, refs = refs[:5], refs[5], refs[6:]
    pooled_ref, pooled_sems, w1_buf, pre1, pre2, act1, act2, pred, w_sems, sems = refs[:-3]
    later = later_copies(w2_ref, wp_ref, *refs[-3:])

    @pl.when(lax.axis_index("section") == 1)
    def _():
        weight_copy(w1_ref, w1_buf, w_sems, 0).start()
        pooled_copies(pooled_ref, parts, pooled_sems, "in", True)
        weight_copy(w1_ref, w1_buf, w_sems, 1).start()

        def ready(piece):
            @pl.when(piece == 0)
            def _():
                pooled_copies(pooled_ref, parts, pooled_sems, "in", False)
                weight_copy(w1_ref, w1_buf, w_sems, 2).start()

            @pl.when(piece + 3 < PIECES)
            def _():
                weight_copy(w1_ref, w1_buf, w_sems, piece + 3).start()

            @pl.when(piece == 3)
            def _():
                for copy in later:
                    copy.start()

        first_layer(pooled_ref, w1_ref, w1_buf, w_sems, b1_ref, pre1, ready)
        for copy in later:
            copy.wait()
        copies = [
            pltpu.make_async_copy(here, there, sems.at[place])
            for place, (here, there) in enumerate(zip((pre1, pre2, act1, act2, pred), kept_out))
        ]
        later_layers(
            1,
            own_records(record_ref, box_ref),
            pre1,
            pre2,
            act1,
            act2,
            pred,
            next_ref,
            refs[-3],
            b2_ref,
            refs[-2],
            bp_ref,
            lambda place: copies[place].start(),
        )
        for copy in copies:
            copy.wait()


def run_head(records, boxes, weights, parts, kept):
    return pl.pallas_call(
        head_kernel,
        out_shape=tuple(jax.ShapeDtypeStruct(*entry) for entry in KEPT)
        + (jax.ShapeDtypeStruct((SLOTS, 128), F32),),
        in_specs=[VMEM] * 3 + [HBM, VMEM, HBM, VMEM] + [HBM] * (1 + 2 * SIDE + 5),
        out_specs=(HBM,) * 5 + (VMEM,),
        scratch_shapes=POOLED_SCRATCH + HEAD_SCRATCH,
        input_output_aliases={8 + 2 * SIDE + place: place for place in range(5)},
        compiler_params=PARAMS,
        cost_estimate=pl.CostEstimate(
            flops=10**10, bytes_accessed=40 * 10**6, transcendentals=6 * 10**5
        ),
        name="run_head",
    )(records, boxes, *weights, *parts, *kept)


def put_parts(values, high_ref, low_ref):
    high = values.astype(BF16)
    high_ref[...] = high
    low_ref[...] = (values - high.astype(F32)).astype(BF16)


def put_tail(target, bias, boxes):
    target[:, 512:] = jnp.zeros((TAIL, target.shape[1] - 512), BF16)
    put_parts(bias, target.at[:, 0:256], target.at[:, 256:512])
    put_parts(boxes, target.at[:, 512:528], target.at[:, 528:544])


def pass_tail(target, bias, back_ref, own):
    target[:, 640:] = jnp.zeros((TAIL, target.shape[1] - 640), BF16)
    put_parts(bias, target.at[:, 0:256], target.at[:, 256:512])
    target[:, 512:640] = back_ref[pl.ds(own, 16, stride=SIDE), :].astype(BF16)


def take_tails(tails, back_ref):
    for k, tail in enumerate(tails):
        back_ref[k * 16 : (k + 1) * 16, :] = tail[:, 512:640].astype(F32)
    near, here, far, across = [
        tail[:, 0:256].astype(F32) + tail[:, 256:512].astype(F32) for tail in tails
    ]
    return (near + far) + (here + across)


def slope_kernel(
    record_ref,
    place_ref,
    next0_ref,
    next1_ref,
    pred,
    pre1,
    pre2,
    act1,
    act2,
    w2_ref,
    wp_ref,
    grad_ref,
    turned_ref,
    c0,
    c1,
    c2,
    c3,
    extra_ref,
    bias_ref,
    back_ref,
    sorted_ref,
):
    own_x, own_z, own_y = coordinates()
    first_section = lax.axis_index("section") == 0
    factor = jnp.where(first_section, 1.0, 0.5).astype(F32)
    records = record_ref[...]
    values = pred[...]
    lane = lax.broadcasted_iota(jnp.int32, values.shape, 1)
    is_class = lane < CLASSES
    peak = jnp.max(jnp.where(is_class, values, -jnp.inf), axis=1, keepdims=True)
    shares = jnp.where(is_class, jnp.exp(values - peak), 0.0)
    shares = shares / jnp.sum(shares, axis=1, keepdims=True)
    label = records[:, LABEL : LABEL + 1]
    weight = factor * records[:, LIVE : LIVE + 1]
    truth = jnp.where(lane.astype(F32) == label, 1.0, 0.0)
    aims = jnp.zeros_like(values)
    for k in range(4):
        aims = jnp.where(lane == CLASSES + k, records[:, TARGET + k : TARGET + k + 1], aims)
    pull = jnp.minimum(jnp.maximum(values - aims, -1.0), 1.0)
    pull = jnp.where(lane < PRED, pull, 0.0) * jnp.where(label > 0.0, 1.0, 0.0)
    out_grad = (jnp.where(is_class, shares - truth, pull) * weight).astype(BF16)
    pred_bias = jnp.sum(out_grad.astype(F32), axis=0, keepdims=True)
    second = jnp.dot(out_grad, wp_ref[...], preferred_element_type=F32)
    second = (second * gelu_slope(pre2[...])).astype(BF16)
    second_bias = jnp.sum(second.astype(F32), axis=0, keepdims=True)
    first = lax.dot_general(
        second, w2_ref[...], (((1,), (1,)), ((), ())), preferred_element_type=F32
    )
    first = (first * gelu_slope(pre1[...])).astype(BF16)
    grad_ref[...] = first
    wide = first.astype(F32)
    first_bias = jnp.sum(wide, axis=0, keepdims=True)
    turned = wide.T.astype(BF16)
    turned_ref[...] = turned
    second_turned = second.astype(F32).T.astype(BF16)
    extra_ref[:, :HIDDEN] = jnp.dot(
        second_turned, act1[...], preferred_element_type=F32
    ).astype(BF16)
    act2_turned = act2[...].astype(F32).T.astype(BF16)
    extra_ref[:, HIDDEN:] = jnp.dot(
        act2_turned, out_grad, preferred_element_type=F32
    ).astype(BF16)
    bias_ref[...] = jnp.zeros_like(bias_ref)
    for row in range(4):
        bias_ref[row : row + 1, :] = first_bias[:, row * 256 : (row + 1) * 256]
        bias_ref[4 + row : 5 + row, :] = second_bias[:, row * 256 : (row + 1) * 256]
    bias_ref[8:9, :128] = pred_bias
    order = jnp.where(
        lax.broadcasted_iota(jnp.int32, (SLOTS, SLOTS), 1).astype(F32) == place_ref[:, 0:1],
        1.0,
        0.0,
    )
    mine = jnp.where(first_section, next0_ref[...], next1_ref[...])
    boxes = jnp.dot(order, mine, precision=EXACT, preferred_element_type=F32)
    small_lane = lax.broadcasted_iota(jnp.int32, (GROUPS, 128), 1)
    back = jnp.zeros((GROUPS, 128), F32)
    for c in range(4):
        for k in range(4):
            back = jnp.where(
                small_lane == 4 * c + k, boxes[c * GROUPS : (c + 1) * GROUPS, k : k + 1], back
            )
    back_ref[...] = back
    for x in range(SIDE):
        for y in range(SIDE):
            sorted_ref[(x * SIDE + y) * SIDE : (x * SIDE + y + 1) * SIDE, :] = back_ref[
                pl.ds(x * 16 + y, SIDE, stride=SIDE), :
            ]
    for jx, target in enumerate((c0, c1, c2, c3)):
        for jz in range(SIDE):
            for jy in range(SIDE):
                source = (
                    (own_x + jx) % SIDE * 256 + (own_z + jz) % SIDE * 64 + (own_y + jy) % SIDE * 16
                )
                to = (jz * SIDE + jy) * 16
                target[to : to + 16, :] = extra_ref[pl.ds(pl.multiple_of(source, 16), 16), :]
        rows = pl.ds(pl.multiple_of((own_x + jx) % SIDE * 16, 16), 16)
        put_tail(target.at[256:, :], bias_ref[...], sorted_ref[rows, :16])


def run_slopes(records, places, after_first, after_second, kept, w2, wp):
    pre1, pre2, act1, act2, pred = kept
    return pl.pallas_call(
        slope_kernel,
        out_shape=(
            jax.ShapeDtypeStruct((SLOTS, HIDDEN), BF16),
            jax.ShapeDtypeStruct((HIDDEN, SLOTS), BF16),
        )
        + (jax.ShapeDtypeStruct((256 + TAIL, EXTRA), BF16),) * SIDE,
        in_specs=[VMEM] * 11,
        out_specs=(VMEM,) * 6,
        scratch_shapes=[
            pltpu.VMEM((HIDDEN, EXTRA), BF16),
            pltpu.VMEM((TAIL, 256), F32),
            pltpu.VMEM((GROUPS, 128), F32),
            pltpu.VMEM((GROUPS, 128), F32),
        ],
        compiler_params=PARAMS,
        cost_estimate=pl.CostEstimate(
            flops=10**6, bytes_accessed=10**5, transcendentals=0
        ),
        name="run_slopes",
    )(records, places, after_first, after_second, pred, pre1, pre2, act1, act2, w2, wp)


def pooled_grad_kernel(grad_ref, w1_ref, out_ref, w1_buf, out_buf, w_sems, out_sems):
    def out_copy(piece):
        columns = pl.ds(pl.multiple_of(piece * PIECE, PIECE), PIECE)
        return pltpu.make_async_copy(out_buf.at[piece], out_ref.at[:, columns], out_sems.at[piece])

    for piece in range(3):
        weight_copy(w1_ref, w1_buf, w_sems, piece).start()

    def one_piece(piece, carry):
        @pl.when(piece + 3 < PIECES)
        def _():
            weight_copy(w1_ref, w1_buf, w_sems, piece + 3).start()

        weight_copy(w1_ref, w1_buf, w_sems, piece).wait()
        rows = pl.ds(pl.multiple_of(piece * PIECE, PIECE), PIECE)
        out_buf[piece] = lax.dot_general(
            grad_ref[...], w1_buf[rows, :], (((1,), (1,)), ((), ())), preferred_element_type=F32
        ).astype(BF16)
        out_copy(piece).start()
        return carry

    lax.fori_loop(0, PIECES, one_piece, 0)

    def finish(piece, carry):
        out_copy(piece).wait()
        return carry

    lax.fori_loop(0, PIECES, finish, 0)


def run_pooled_grad(grad, w1):
    return pl.pallas_call(
        pooled_grad_kernel,
        out_shape=jax.ShapeDtypeStruct((SLOTS, FEATURES), BF16),
        in_specs=[VMEM, HBM],
        out_specs=HBM,
        scratch_shapes=[
            pltpu.VMEM((FEATURES, HIDDEN), BF16),
            pltpu.VMEM((PIECES, SLOTS, PIECE), BF16),
            pltpu.SemaphoreType.DMA((PIECES,)),
            pltpu.SemaphoreType.DMA((PIECES,)),
        ],
        compiler_params=PARAMS,
        cost_estimate=pl.CostEstimate(
            flops=2 * SLOTS * FEATURES * HIDDEN, bytes_accessed=33 * 10**6, transcendentals=0
        ),
        name="run_pooled_grad",
    )(grad, w1)


def scatter_kernel(
    count_ref,
    record_ref,
    box_ref,
    table_ref,
    grad_ref,
    out_ref,
    coord_ref,
    spread_ref,
    turned_ref,
    rows_ref,
    grad_buf,
    slot_ref,
    wide_ref,
    sems,
):
    up_to = [count_ref[octave] for octave in range(4)]
    lane = lax.broadcasted_iota(jnp.int32, (1, 128), 1)
    lane_bin = lane // GROUP

    def grad_copy(quarter):
        rows = pl.ds(pl.multiple_of(quarter * SLOT_QUARTER, SLOT_QUARTER), SLOT_QUARTER)
        return pltpu.make_async_copy(grad_ref.at[rows, :], grad_buf.at[rows, :], sems.at[quarter])

    for quarter in range(SIDE):
        grad_copy(quarter).start()
    out_ref[...] = jnp.zeros_like(out_ref)
    rows_ref[...] = jnp.zeros_like(rows_ref)
    records = record_ref[...]
    wide_lane = lax.broadcasted_iota(jnp.int32, records.shape, 1)
    passed = (wide_lane < 4) & (lax.axis_index("section") == 1)
    records = jnp.where(passed, box_ref[...], records)
    coords = sample_coordinates(records)
    coords = jnp.where(wide_lane == 32, records[:, LEVEL : LEVEL + 1], coords)
    slot_ref[...] = coords
    left = coords.T[:48, :]
    repeat = jnp.where(
        lax.broadcasted_iota(jnp.int32, (SLOTS, 2048), 0)
        == lax.broadcasted_iota(jnp.int32, (SLOTS, 2048), 1) // 128 * GROUP
        + lax.broadcasted_iota(jnp.int32, (SLOTS, 2048), 1) % GROUP,
        1.0,
        0.0,
    ).astype(BF16)
    wide = jnp.zeros((48, 2048), F32)
    for _ in range(3):
        part = left.astype(BF16)
        left = left - part.astype(F32)
        wide = wide + jnp.dot(part, repeat, preferred_element_type=F32)
    wide_ref[...] = wide

    def one_quarter(quarter, carry):
        grad_copy(quarter).wait()
        first = quarter * (SLOT_QUARTER // GROUP)
        live = (up_to[3] + GROUP - 1) // GROUP
        lax.fori_loop(first, jnp.minimum(first + SLOT_QUARTER // GROUP, live), one_group, 0)
        return carry

    def one_group(group, carry):
        start = pl.multiple_of(group * GROUP, GROUP)
        coords = slot_ref[pl.ds(start, GROUP), :]
        coord_ref[...] = wide_ref[:, pl.ds(pl.multiple_of(group * 128, 128), 128)]
        for p in range(7):
            for q in range(7):
                spot = p * 7 + q
                rows_ref[p * 128 + q * GROUP : p * 128 + (q + 1) * GROUP, :] = grad_buf[
                    pl.ds(start, GROUP), spot * CHANNELS : (spot + 1) * CHANNELS
                ]

        def column_ends():
            ends = []
            for side in range(2):
                value = jnp.full((1, 128), -2000.0, F32)
                for q in range(7):
                    row = 16 + 2 * q + side
                    value = jnp.where(lane_bin == q, coord_ref[row : row + 1, :], value)
                ends.append(value)
            return ends

        def ends_of_row(p):
            return coord_ref[2 * p : 2 * p + 1, :], coord_ref[2 * p + 1 : 2 * p + 2, :]

        def grid_block(height, first_row):
            width = 48
            left, right = column_ends()
            wanted = coord_ref[32:33, :] == 0.0
            x_cells = 0.5 * lax.broadcasted_iota(jnp.int32, (width, 128), 0).astype(F32)
            y_cells = 0.5 * (
                lax.broadcasted_iota(jnp.int32, (height, 128), 0) + first_row
            ).astype(F32)
            columns = jnp.where(wanted, tent_pair(left, right, x_cells), 0.0)
            cells = height * width
            for p in range(7):
                top, bottom = ends_of_row(p)
                spread_ref[:height, :] = tent_pair(top, bottom, y_cells)
                for y in range(height):
                    turned_ref[y * width : (y + 1) * width, p * 128 : (p + 1) * 128] = (
                        spread_ref[y : y + 1, :] * columns
                    ).astype(BF16)
            out_ref[pl.ds(pl.multiple_of(first_row * 48, 16), cells), :] += jnp.dot(
                turned_ref[:cells, :], rows_ref[...], preferred_element_type=F32
            )

        @pl.when(start < up_to[0])
        def _():
            first, count = row_window(coords, coords[:, 32:33] == 0.0)

            @pl.when(count <= 10)
            def _():
                grid_block(10, jnp.minimum(first, 22))

            @pl.when((count > 10) & (count <= 20))
            def _():
                grid_block(20, jnp.minimum(first, 12))

            @pl.when(count > 20)
            def _():
                grid_block(32, jnp.int32(0))

        @pl.when((start + GROUP > up_to[0]) & (start < up_to[1]))
        def _():
            left, right = column_ends()
            wanted = coord_ref[32:33, :] == 1.0
            x_cells = 0.5 * lax.broadcasted_iota(jnp.int32, (24, 128), 0).astype(F32)
            y_cells = 0.5 * lax.broadcasted_iota(jnp.int32, (16, 128), 0).astype(F32)
            columns = jnp.where(wanted, tent_pair(left, right, x_cells), 0.0)
            for p in range(7):
                top, bottom = ends_of_row(p)
                spread_ref[:16, :] = tent_pair(top, bottom, y_cells)
                for y in range(0, 16, 2):
                    both = jnp.concatenate(
                        [spread_ref[y : y + 1, :] * columns, spread_ref[y + 1 : y + 2, :] * columns],
                        axis=0,
                    )
                    turned_ref[y * 24 : (y + 2) * 24, p * 128 : (p + 1) * 128] = both.astype(BF16)
            out_ref[1536:1920, :] += jnp.dot(
                turned_ref[:384, :], rows_ref[...], preferred_element_type=F32
            )

        @pl.when((start + GROUP > up_to[1]) & (start < up_to[3]))
        def _():
            left, right = column_ends()
            y_cells = table_ref[:, 0:1]
            x_cells = table_ref[:, 1:2]
            wanted = coord_ref[32:33, :] == table_ref[:, 2:3]
            columns = jnp.where(wanted, tent_pair(left, right, x_cells), 0.0)
            for p in range(7):
                top, bottom = ends_of_row(p)
                turned_ref[:128, p * 128 : (p + 1) * 128] = (
                    tent_pair(top, bottom, y_cells) * columns
                ).astype(BF16)
            update = jnp.dot(turned_ref[:128, :], rows_ref[...], preferred_element_type=F32)
            out_ref[1920:CELLS, :] += update[: CELLS - 1920, :]

        return carry

    lax.fori_loop(0, SIDE, one_quarter, 0)


def run_scatter(counts, records, boxes, table, pooled_grad):
    return pl.pallas_call(
        scatter_kernel,
        out_shape=jax.ShapeDtypeStruct((CELLS, CHANNELS), F32),
        in_specs=[SMEM, VMEM, VMEM, VMEM, HBM],
        out_specs=VMEM,
        scratch_shapes=[
            pltpu.VMEM((48, 128), F32),
            pltpu.VMEM((32, 128), F32),
            pltpu.VMEM((1536, 7 * 128), BF16),
            pltpu.VMEM((7 * 128, CHANNELS), BF16),
            pltpu.VMEM((SLOTS, FEATURES), BF16),
            pltpu.VMEM((SLOTS, 128), F32),
            pltpu.VMEM((48, 2048), F32),
            pltpu.SemaphoreType.DMA((SIDE,)),
        ],
        compiler_params=PARAMS,
        cost_estimate=pl.CostEstimate(
            flops=2 * 10**10, bytes_accessed=9 * 10**6, transcendentals=0
        ),
        name="run_scatter",
    )(counts, records, boxes, table, pooled_grad)


def load_pieces(turned_in, gained, pooled, turned, right, sems, piece_sems, steps):
    sources = [turned_in, *gained]
    first = [
        pltpu.make_async_copy(source, turned.at[k], sems.at[k]) for k, source in enumerate(sources)
    ]
    later = [
        [
            pltpu.make_async_copy(
                pooled[k].at[:, start : start + width],
                right.at[pl.ds(k * SLOTS, SLOTS), start : start + width],
                piece_sems.at[step, k],
            )
            for k in range(SIDE)
        ]
        for step, (start, width) in enumerate(steps)
    ]
    for copy in first:
        copy.start()
    for copies in later:
        for copy in copies:
            copy.start()
    return first, later


def place_left(left, turned, row_of):
    own_x, own_z, own_y = coordinates()
    for j in range(SIDE):
        for i in range(SIDE):
            for h in range(SIDE):
                jx, jz, jy = row_of(j, i, h)
                source = (
                    (own_x + jx) % SIDE * 256 + (own_z + jz) % SIDE * 64 + (own_y + jy) % SIDE * 16
                )
                to = ((j * SIDE + i) * SIDE + h) * 16
                for k in range(SIDE):
                    left[to : to + 16, k * SLOTS : (k + 1) * SLOTS] = turned[
                        k, pl.ds(pl.multiple_of(source, 16), 16), :
                    ]


def multiply(left, right, part, start, width):
    def one(step, carry):
        columns = pl.ds(pl.multiple_of(start + step * 256, 128), 256)
        value = jnp.dot(left[...], right[:, columns], preferred_element_type=F32).astype(BF16)
        for j in range(SIDE):
            part[j, :256, columns] = value[j * 256 : (j + 1) * 256, :]
        return carry

    lax.fori_loop(0, width // 256, one, 0)
    if width % 256:
        end = start + width
        value = jnp.dot(
            left[...], right[:, end - 128 : end], preferred_element_type=F32
        ).astype(BF16)
        for j in range(SIDE):
            part[j, :256, end - 128 : end] = value[j * 256 : (j + 1) * 256, :]


STEPS_Y = ((0, 512), (512, 512))
STEPS_Z = ((0, 1024), (1024, 1152))


def weight_grad_kernel(steps, row_of, extra_count, *refs):
    turned_in, gained, pooled = refs[0], refs[1:4], refs[4:8]
    extras, refs = refs[8 : 8 + extra_count], refs[8 + extra_count :]
    outs, (turned, right, left, part, sems, piece_sems, out_sems) = refs[:SIDE], refs[SIDE:]
    added = [
        pltpu.make_async_copy(extra, part.at[j, :, PART_Y:], out_sems.at[SIDE + j])
        for j, extra in enumerate(extras)
    ]
    for copy in added:
        copy.start()
    first, later = load_pieces(turned_in, gained, pooled, turned, right, sems, piece_sems, steps)
    for copy in first:
        copy.wait()
    place_left(left, turned, row_of)
    for copies, (start, width) in zip(later, steps):
        for copy in copies:
            copy.wait()
        multiply(left, right, part, start, width)
    for copy in added:
        copy.wait()
    results = [pltpu.make_async_copy(part.at[j], outs[j], out_sems.at[j]) for j in range(SIDE)]
    for copy in results:
        copy.start()
    for copy in results:
        copy.wait()


def run_weight_grad(name, steps, row_of, turned, gained, pooled, extra=()):
    width = pooled[0].shape[1]
    shape = (256 + TAIL, width + EXTRA) if extra else (256, width)
    return pl.pallas_call(
        lambda *refs: weight_grad_kernel(steps, row_of, len(extra), *refs),
        out_shape=(jax.ShapeDtypeStruct(shape, BF16),) * SIDE,
        in_specs=[HBM] * (8 + len(extra)),
        out_specs=(HBM,) * SIDE,
        scratch_shapes=[
            pltpu.VMEM((SIDE, HIDDEN, SLOTS), BF16),
            pltpu.VMEM((HIDDEN, width), BF16),
            pltpu.VMEM((HIDDEN, HIDDEN), BF16),
            pltpu.VMEM((SIDE, *shape), BF16),
            pltpu.SemaphoreType.DMA((SIDE,)),
            pltpu.SemaphoreType.DMA((len(steps), SIDE)),
            pltpu.SemaphoreType.DMA((2 * SIDE,)),
        ],
        compiler_params=PARAMS,
        cost_estimate=pl.CostEstimate(
            flops=3 * HIDDEN * HIDDEN * width, bytes_accessed=9 * 10**6, transcendentals=0
        ),
        name=name,
    )(turned, *gained, *pooled, *extra)


def add_rows(ins, rows):
    total = ins[0][rows, :].astype(F32)
    for k in range(1, SIDE):
        total += ins[k][rows, :].astype(F32)
    return total


def sum_y_first_kernel(*refs):
    ins, outs, back_ref = refs[:SIDE], refs[SIDE : 2 * SIDE], refs[2 * SIDE]
    own_x, own_z, own_y = coordinates()
    bias = take_tails([part.at[256:, PART_Y:] for part in ins], back_ref)
    for j in range(SIDE):
        outs[j][:64, :] = add_rows(ins, slice(64 * j, 64 * (j + 1))).astype(BF16)
        outs[j][64:, :PART_Y] = jnp.zeros((TAIL, PART_Y), BF16)
        pass_tail(outs[j].at[64:, PART_Y:], bias, back_ref, (own_z + j) % SIDE)


def sum_y_first(parts):
    return pl.pallas_call(
        sum_y_first_kernel,
        out_shape=(jax.ShapeDtypeStruct((64 + TAIL, WIDE_Y), BF16),) * SIDE,
        in_specs=[VMEM] * SIDE,
        out_specs=(VMEM,) * SIDE,
        scratch_shapes=[pltpu.VMEM((GROUPS, 128), F32)],
        compiler_params=SMALL,
        cost_estimate=pl.CostEstimate(flops=10**6, bytes_accessed=4 * 10**6, transcendentals=0),
        name="sum_y_first",
    )(*parts)


def sum_y_second_kernel(*refs):
    ins, outs, back_ref = refs[:SIDE], refs[SIDE : 2 * SIDE], refs[2 * SIDE]
    own_x, own_z, own_y = coordinates()
    bias = take_tails([part.at[64:, PART_Y:] for part in ins], back_ref)
    for j in range(SIDE):
        outs[j][:16, :] = add_rows(ins, slice(16 * j, 16 * (j + 1))).astype(BF16)
        outs[j][16:, :PART_Y] = jnp.zeros((TAIL, PART_Y), BF16)
        pass_tail(outs[j].at[16:, PART_Y:], bias, back_ref, (own_y + j) % SIDE)


def sum_y_second(parts):
    return pl.pallas_call(
        sum_y_second_kernel,
        out_shape=(jax.ShapeDtypeStruct((16 + TAIL, WIDE_Y), BF16),) * SIDE,
        in_specs=[VMEM] * SIDE,
        out_specs=(VMEM,) * SIDE,
        scratch_shapes=[pltpu.VMEM((GROUPS, 128), F32)],
        compiler_params=SMALL,
        cost_estimate=pl.CostEstimate(flops=10**6, bytes_accessed=10**6, transcendentals=0),
        name="sum_y_second",
    )(*parts)


def sum_z_kernel(rows, *refs):
    ins, outs = refs[:SIDE], refs[SIDE:]
    for j in range(SIDE):
        outs[j][...] = add_rows(ins, slice(rows * j, rows * (j + 1))).astype(BF16)


def sum_z(parts):
    rows = parts[0].shape[0] // SIDE
    return pl.pallas_call(
        lambda *refs: sum_z_kernel(rows, *refs),
        out_shape=(jax.ShapeDtypeStruct((rows, PART_Z), BF16),) * SIDE,
        in_specs=[VMEM] * SIDE,
        out_specs=(VMEM,) * SIDE,
        compiler_params=SMALL,
        cost_estimate=pl.CostEstimate(flops=10**6, bytes_accessed=10**6, transcendentals=0),
        name="sum_z",
    )(*parts)


def join_kernel(image_ref, *refs):
    parts_y, parts_z = refs[:SIDE], refs[SIDE : 2 * SIDE]
    out_ref, second_ref, pred_ref, first_bias, second_bias, pred_bias, refined_ref = refs[
        2 * SIDE : 2 * SIDE + 7
    ]
    back_ref, bias_ref = refs[2 * SIDE + 7 :]
    own_x, own_z, own_y = coordinates()
    for parts, own, width, first in (
        (parts_y, own_y, PART_Y, 0),
        (parts_z, own_z, PART_Z, SPLIT),
    ):
        for k in range(SIDE):
            for chunk in range(SIDE):
                start = first + chunk * width
                count = min(width, FEATURES - start)

                @pl.when((own - k + SIDE) % SIDE == chunk)
                def _():
                    out_ref[:, start : start + count] = parts[k][:16, :count].astype(F32)

    extra = [part.at[:, PART_Y:] for part in parts_y]
    total = add_rows(extra, slice(0, 16))
    second_ref[...] = total[:, :HIDDEN]
    pred_ref[...] = total[:, HIDDEN:]
    bias_ref[...] = take_tails([part.at[16:, :] for part in extra], back_ref)
    for row in range(4):
        lanes = slice(row * 256, (row + 1) * 256)
        first_bias[:, lanes] = bias_ref[row : row + 1, :]
        second_bias[:, lanes] = bias_ref[4 + row : 5 + row, :]
    pred_bias[...] = bias_ref[8:9, :128]
    images = image_ref[...]
    slot = slot_of_regions(images.astype(F32))
    owner = (
        jnp.bitwise_and(own_y - images, 3) * 16
        + jnp.bitwise_and(own_z - (images >> 2), 3) * 4
        + jnp.bitwise_and(own_x - (images >> 4), 3)
    )
    chosen = jnp.where(lax.broadcasted_iota(jnp.int32, (GROUPS, REGIONS), 0) == owner, 1.0, 0.0)
    values = jnp.dot(back_ref[...].T, chosen, precision=EXACT, preferred_element_type=F32)
    values = values[:16, :] + values[16:32, :]
    result = jnp.zeros((4, REGIONS), F32)
    for c in range(4):
        result = jnp.where(slot == float(c), values[4 * c : 4 * c + 4, :], result)
    refined_ref[...] = result


def join_parts(images, parts_y, parts_z):
    return pl.pallas_call(
        join_kernel,
        out_shape=(
            jax.ShapeDtypeStruct((16, FEATURES), F32),
            jax.ShapeDtypeStruct((16, HIDDEN), F32),
            jax.ShapeDtypeStruct((16, 128), F32),
            jax.ShapeDtypeStruct((1, HIDDEN), F32),
            jax.ShapeDtypeStruct((1, HIDDEN), F32),
            jax.ShapeDtypeStruct((1, 128), F32),
            jax.ShapeDtypeStruct((4, REGIONS), F32),
        ),
        in_specs=[VMEM] * (1 + 2 * SIDE),
        out_specs=(VMEM,) * 7,
        scratch_shapes=[pltpu.VMEM((GROUPS, 128), F32), pltpu.VMEM((TAIL, 256), F32)],
        compiler_params=SMALL,
        cost_estimate=pl.CostEstimate(flops=10**6, bytes_accessed=2 * 10**6, transcendentals=0),
        name="join_parts",
    )(images, *parts_y, *parts_z)


def ring(arrays, axis):
    return [arrays[0]] + [shift(arrays[by], axis, by) for by in range(1, SIDE)]


def body(
    pyramid,
    boxes,
    image_ids,
    levels,
    labels,
    targets,
    w_first,
    b_first,
    w_second,
    b_second,
    w_pred,
    b_pred,
):
    rows, cols, cell_levels = cell_tables()
    lane_table = jnp.asarray(np.stack([rows, cols, cell_levels] + [np.zeros_like(rows)] * 5))
    side_table = np.zeros((128, 128), np.float32)
    side_table[:, 0], side_table[:, 1], side_table[:, 2] = (
        rows[1920:],
        cols[1920:],
        cell_levels[1920:],
    )
    side_table = jnp.asarray(side_table)
    feature_map = jnp.pad(pyramid[0], ((0, CELLS_PAD - CELLS), (0, 0)))
    pred_weight = jnp.pad(w_pred[0], ((0, 128 - PRED), (0, 0)))
    pred_bias = jnp.pad(b_pred, ((0, 0), (0, 128 - PRED)))
    image_row = image_ids.reshape(1, REGIONS)

    with jax.named_scope("regions_to_images"):
        sent = send_regions(image_row, boxes, levels.reshape(1, REGIONS), labels, targets[0])
        got = lax.all_to_all(sent, "region", 0, 0, tiled=True)
    records, places, counts = select_slots(got)
    weights = (b_first, w_second[0], b_second, pred_weight, pred_bias, w_first[0])

    *kept, after_first = run_forward(counts, records, feature_map, lane_table, weights)
    with jax.named_scope("boxes_to_second"):
        passed = lax.ppermute(after_first, "section", [(0, 1)])
    kept, pooled = kept[2 * SIDE :], kept[: 2 * SIDE]
    pooled = run_pool(counts, records, passed, feature_map, lane_table, pooled)
    with jax.named_scope("pooled_over_rings"):
        pooled_y = ring(pooled[:SIDE], "y")
        pooled_z = [pooled[SIDE]] + [shift(pooled[SIDE + by], "z", by) for by in (1, 3)]
    *kept, after_second = run_head(records, passed, weights, pooled, kept)
    grad, turned, *extra = run_slopes(
        records, places, after_first, after_second, kept, w_second[0], pred_weight
    )
    *joined, last, grad = lax.optimization_barrier(
        (*pooled_y, *pooled_z, pooled[SIDE + 2], grad)
    )
    pooled_y, pooled_z = joined[:SIDE], joined[SIDE:]
    with jax.named_scope("pooled_over_rings"):
        pooled_z.insert(2, shift(last, "z", 2))
    with jax.named_scope("gradient_over_rings"):
        gained_y = ring([turned] * SIDE, "y")[1:]
        gained_z = [shift(turned, "z", 1)]
    pooled_grad = run_pooled_grad(grad, w_first[0])
    *gained_z, pooled_z[2], pooled_grad, turned = lax.optimization_barrier(
        (*gained_z, pooled_z[2], pooled_grad, turned)
    )
    with jax.named_scope("gradient_over_rings"):
        gained_z += [shift(turned, "z", by) for by in (2, 3)]
    part_y = run_weight_grad(
        "run_grad_y", STEPS_Y, lambda j, i, h: (j, i, h), turned, gained_y, pooled_y, extra
    )
    *part_y, turned = lax.optimization_barrier((*part_y, turned))
    part_z = run_weight_grad(
        "run_grad_z", STEPS_Z, lambda j, i, h: (i, h, j), turned, gained_z, pooled_z
    )
    *part_z, pooled_grad = lax.optimization_barrier((*part_z, pooled_grad))
    map_grad = run_scatter(counts, records, passed, side_table, pooled_grad)
    with jax.named_scope("sum_over_rings"):
        part_y, part_z = ring(part_y, "x"), ring(part_z, "y")
        part_y[0], part_z[0], map_grad = lax.optimization_barrier((part_y[0], part_z[0], map_grad))
        part_y = ring(sum_y_first(part_y), "z")
        part_z = ring(sum_z(part_z), "x")
        part_y, part_z = sum_y_second(part_y), sum_z(part_z)
    with jax.named_scope("columns_over_rings"):
        first, second, pred, first_bias, second_bias, bias, refined = join_parts(
            image_row, ring(part_y, "y"), ring(part_z, "z")
        )
    return (
        first.T[None],
        first_bias,
        second.T[None],
        second_bias,
        pred[:, :PRED].T[None],
        bias[:, :PRED],
        map_grad[None, None],
        refined[None],
    )


def solution(mesh):
    return jax.shard_map(
        body,
        mesh=mesh,
        in_specs=(
            P("region", None, None),
            P(None, "region"),
            P("region", None),
            P("region"),
            P("section", "region"),
            P("section", None, "region"),
            P("section", None, None),
            P("section", None),
            P("section", None, None),
            P("section", None),
            P("section", None, None),
            P("section", None),
        ),
        out_specs=(
            P("section", None, "region"),
            P("section", None),
            P("section", None, "region"),
            P("section", None),
            P("section", None, "region"),
            P("section", None),
            P("section", "region", None, None),
            P("section", None, "region"),
        ),
        check_vma=False,
    )
```
